512 devices in a mesh: dp: 16 (over y_lo, x, core), expert: 32 (over z, y_hi).
Axes of the slice: x: 4, y: 4 (y_hi: 2, y_lo: 2; y = y_hi * 2 + y_lo), z: 16, core: 2. Of those that a mesh axis runs over, the one named last changes fastest.
Arguments:
- tokens: bfloat16 [65536, 2048], P(('dp', 'expert')), may hold values from -6 to 6
- target: bfloat16 [65536, 2048], P(('dp', 'expert')), may hold values from -6 to 6
- routes: int32 [65536, 2], P(('dp', 'expert')), may hold values from 0 to 15, all different within a row; in each aligned block of 128 rows (0 to 127, 128 to 255, ...) at most 20 rows name the same one
- gates: float32 [65536, 2], P(('dp', 'expert')), may hold values from 0.2 to 0.8
- w_gate: bfloat16 [2048, 12288], P('dp', 'expert'), may hold values from -0.125 to 0.125
- w_up: bfloat16 [2048, 12288], P('dp', 'expert'), may hold values from -0.125 to 0.125
- w_down: bfloat16 [12288, 2048], P('expert', 'dp'), may hold values from -0.21875 to 0.21875
- error: bfloat16 [196608, 2048], P(('dp', 'expert')), may hold values from -6 to 6
- q_start: float32 [2048, 512], P(None, 'expert'), may hold values from -6 to 6
Outputs:
- token_grad: bfloat16 [65536, 2048], P(('dp', 'expert'))
- p_factor: float32 [12288, 32], P('expert')
- q_factor: float32 [2048, 512], P('dp', 'expert')
- new_error: bfloat16 [196608, 2048], P(('dp', 'expert'))
The draws below stay inside these ranges and needn't reach their ends.
Inputs may be any that keep to these rules, and one draw needn't show every extreme that they name: `routes`: each token names 2 different experts; in the 128 rows of one device no expert is named more than 20 times, a bound that some block reaches.
All inputs are finite; a program needn't handle non-finite values.
Results may differ from the reference program's by a relative error of at most 0.0085.
Values may be sent and summed in bfloat16 or wider, within the bound.
No kernel may reach another device: no remote copies, remote signals or barrier semaphores. Data moves between devices by JAX's collectives and lax.ppermute only.
A program may use at most 64 MiB of HBM per device.

```python
import math
import jax
import jax.numpy as jnp
import numpy as np
from jax import lax

D = 2048
F = 768
R = 32
TOP = 2
TOK_DEV = 128
EXPERTS = 16
HALF = 384
CAP = 20
GROUP_TOK = 4096
TOKENS = 65536
N_DP = 16


def levels(stream_key, shape, shards, smallest, top_value):
    gain, own = 1.0, jax.random.fold_in(stream_key, 6)
    for position, shards_of in shards:
        heights = jnp.exp(jax.random.uniform(jax.random.fold_in(own, position), (shards_of,), jnp.float32, smallest / len(shards), top_value / len(shards)))
        gain = gain * jnp.repeat(heights, shape[position] // shards_of).reshape([-1 if axis == position else 1 for axis in range(len(shape))])
    return gain


def assign_block(rng, own, number, rows, count, top, bound, skew):
    sequence = jax.random.permutation(rng, count)
    crowded, common = portions_of(count, rows * top, bound, skew, True), portions_of(count, rows * top, bound, skew, False)
    places = jnp.arange(count)

    def named(lengths, offset_by):
        used = int((lengths > 0).sum())
        fixed = max(1, used // 4)
        passed = fixed + (places - fixed + offset_by * (used - fixed)) % max(1, count - fixed)
        return jnp.zeros((count,), jnp.int32).at[sequence[jnp.where(places < fixed, places, passed)]].set(jnp.asarray(lengths, jnp.int32))

    lengths = jnp.where(number % 4 == 0, named(crowded, number // 4), named(common, number - number // 4 - 1))
    mixed = jax.random.permutation(jax.random.fold_in(own, 3), count)
    source_of, sink = mixed[0:count // 2 * 2:2], mixed[1:count // 2 * 2:2]
    margin = jnp.minimum(lengths[source_of] - 1, bound - lengths[sink]) // 2
    margin = jnp.where((source_of == sequence[0]) | (sink == sequence[0]) | (lengths[sink] == 0), 0, jnp.maximum(margin, 0))
    passed = jax.random.randint(jax.random.fold_in(own, 4), (count // 2,), 0, 1 << 20) % (margin + 1)
    lengths = lengths.at[source_of].add(-passed).at[sink].add(passed)
    labels = jnp.searchsorted(jnp.cumsum(lengths), jnp.arange(rows * top), side="right").astype(jnp.int32)
    listing = labels.reshape(top, rows).T
    listing = listing[jax.random.permutation(jax.random.fold_in(own, 1), rows)]
    offset_by = jax.random.randint(jax.random.fold_in(own, 2), (rows, 1), 0, top)
    return jnp.take_along_axis(listing, (jnp.arange(top)[None, :] + offset_by) % top, axis=1)


def portions_of(count, total, bound, lean, full):
    loads = [(1 << 20) // math.isqrt(rank ** lean) + 1 for rank in range(1, count + 1)]
    largest = bound if full else min(bound, max(-(-total // count), total * loads[0] // sum(loads)))
    least = 1 if total - largest >= count - 1 else 0
    given, rest = [largest] + [least] * (count - 1), total - largest - least * (count - 1)
    while rest > 0:
        free = [i for i in range(1, count) if given[i] < largest] or [i for i in range(1, count) if given[i] < bound]
        whole, left = sum([loads[i] for i in free]), rest
        for i in free:
            extra = min(bound - given[i], max(1, left * loads[i] // whole), rest)
            given[i] = given[i] + extra
            rest = rest - extra
    return np.array(given)


def centred(key, dims, spread, most, shards=(), kind=jnp.bfloat16):
    values = spread * jax.random.normal(key, dims, jnp.float32)
    if shards:
        values = values * levels(key, dims, shards, -0.22, 0.18)
    return jnp.clip(values, -most, most).astype(kind)


def setup_inputs(seed: int = 0) -> dict:
    key_of = jax.random.split(jax.random.key(seed), 10)
    tokens = centred(key_of[0], (TOKENS, D), 1.0, 6.0, ((0, 512),))
    target = centred(key_of[1], (TOKENS, D), 1.0, 6.0, ((0, 512),))
    routes_keys = jax.random.split(jax.random.fold_in(key_of[2], 1), TOKENS // TOK_DEV)
    routes_turns = jax.random.permutation(jax.random.fold_in(key_of[2], 3), TOKENS // TOK_DEV)
    routes = jax.vmap(lambda own, number: assign_block(jax.random.fold_in(key_of[2], 2), own, number, TOK_DEV, EXPERTS, TOP, CAP, 2))(routes_keys, routes_turns).reshape((TOKENS, TOP))
    gates = jnp.clip(0.2 + 0.6 * jax.random.uniform(key_of[3], (TOKENS, TOP), jnp.float32) ** levels(key_of[3], (TOKENS, TOP), ((0, 512),), -0.2, 0.2), 0.2, 0.8)
    w_gate = centred(key_of[4], (D, EXPERTS * F), D ** -0.5, 0.125, ((0, 16), (1, 32)))
    w_up = centred(key_of[5], (D, EXPERTS * F), D ** -0.5, 0.125, ((0, 16), (1, 32)))
    w_down = centred(key_of[6], (EXPERTS * F, D), F ** -0.5, 0.21875, ((0, 32), (1, 16)))
    error = centred(key_of[7], (N_DP * EXPERTS * F, D), 1.0, 6.0, ((0, 512),))
    q_start = centred(key_of[8], (D, EXPERTS * R), 1.0, 6.0, ((1, 32),), jnp.float32)
    return {"tokens": tokens, "target": target, "routes": routes, "gates": gates, "w_gate": w_gate, "w_up": w_up, "w_down": w_down, "error": error, "q_start": q_start}


def replica_step(rows, goal, route_ids, weights, err, w_gate, w_up, w_down):
    expert_ids = jnp.arange(EXPERTS, dtype=jnp.int32)
    table = jnp.sum(weights[:, :, None] * (route_ids[:, :, None] == expert_ids).astype(jnp.float32), axis=1)
    routed = jnp.sum((route_ids[:, :, None] == expert_ids).astype(jnp.float32), axis=1)

    def forward(index):
        hid_list, gate_list, up_list, part_list = ([], [], [], [])
        for side in range(2):
            start = (index * F + side * HALF).astype(jnp.int32)
            gate_cols = lax.dynamic_slice_in_dim(w_gate, start, HALF, 1)
            up_cols = lax.dynamic_slice_in_dim(w_up, start, HALF, 1)
            down_part = lax.dynamic_slice_in_dim(w_down, start, HALF, 0)
            pre_gate = jnp.dot(rows.astype(jnp.float32), gate_cols.astype(jnp.float32), preferred_element_type=jnp.float32)
            pre_up = jnp.dot(rows.astype(jnp.float32), up_cols.astype(jnp.float32), preferred_element_type=jnp.float32)
            hidden = (jax.nn.silu(pre_gate) * pre_up).astype(jnp.bfloat16)
            part = jnp.dot(hidden.astype(jnp.float32), down_part.astype(jnp.float32), preferred_element_type=jnp.float32).astype(jnp.bfloat16)
            hid_list.append(hidden)
            gate_list.append(pre_gate)
            up_list.append(pre_up)
            part_list.append(part)
        total = (part_list[0].astype(jnp.float32) + part_list[1].astype(jnp.float32)).astype(jnp.bfloat16)
        total = lax.optimization_barrier(total)
        return (jnp.stack(hid_list), jnp.stack(gate_list), jnp.stack(up_list), total)
    hiddens, pre_gates, pre_ups, outs = lax.map(forward, expert_ids)
    layer_sum = jnp.einsum('te,etd->td', table, outs.astype(jnp.float32))
    slope = layer_sum - goal.astype(jnp.float32)

    def backward(items):
        index, hid, pre_gate, pre_up = items
        column = lax.dynamic_slice_in_dim(table, index, 1, 1)
        out_grad = (column * slope).astype(jnp.bfloat16)
        parts, grads = ([], [])
        for side in range(2):
            start = (index * F + side * HALF).astype(jnp.int32)
            gate_cols = lax.dynamic_slice_in_dim(w_gate, start, HALF, 1)
            up_cols = lax.dynamic_slice_in_dim(w_up, start, HALF, 1)
            down_part = lax.dynamic_slice_in_dim(w_down, start, HALF, 0)
            hidden_grad = jnp.dot(out_grad.astype(jnp.float32), down_part.T.astype(jnp.float32), preferred_element_type=jnp.float32)
            grads.append(jnp.dot(hid[side].T.astype(jnp.float32), out_grad.astype(jnp.float32), preferred_element_type=jnp.float32))
            sig = jax.nn.sigmoid(pre_gate[side])
            act = pre_gate[side] * sig
            gate_grad = (hidden_grad * pre_up[side] * sig * (1.0 + pre_gate[side] * (1.0 - sig))).astype(jnp.bfloat16)
            up_grad = (hidden_grad * act).astype(jnp.bfloat16)
            part = jnp.dot(gate_grad.astype(jnp.float32), gate_cols.T.astype(jnp.float32), preferred_element_type=jnp.float32)
            part = part + jnp.dot(up_grad.astype(jnp.float32), up_cols.T.astype(jnp.float32), preferred_element_type=jnp.float32)
            parts.append(part.astype(jnp.bfloat16))
        slot = (parts[0].astype(jnp.float32) + parts[1].astype(jnp.float32)).astype(jnp.bfloat16)
        slot = lax.optimization_barrier(slot)
        return (slot, jnp.concatenate(grads, axis=0))
    slots, weight_grads = lax.map(backward, (expert_ids, hiddens, pre_gates, pre_ups))
    token_grad = jnp.einsum('te,etd->td', routed, slots.astype(jnp.float32)).astype(jnp.bfloat16)
    merged = weight_grads.reshape(EXPERTS * F, D) + err.astype(jnp.float32)
    return (token_grad, merged)

def reference(tokens, target, routes, gates, w_gate, w_up, w_down, error, q_start):

    def replica(items):
        rows, goal, route_ids, weights, err = items
        return replica_step(rows, goal, route_ids, weights, err, w_gate, w_up, w_down)
    token_grad, merged = lax.map(replica, (tokens.reshape(N_DP, GROUP_TOK, D), target.reshape(N_DP, GROUP_TOK, D), routes.reshape(N_DP, GROUP_TOK, TOP), gates.reshape(N_DP, GROUP_TOK, TOP), error.reshape(N_DP, EXPERTS * F, D)))
    highest = lax.Precision.HIGHEST

    def compress(index):
        block = lax.dynamic_slice_in_dim(merged, (index * F).astype(jnp.int32), F, 1)
        start = lax.dynamic_slice_in_dim(q_start, (index * R).astype(jnp.int32), R, 1)
        left = jnp.einsum('gfd,dr->fr', block, start, precision=highest)
        gram = jnp.dot(left.T, left, precision=highest)
        lower = jnp.linalg.cholesky(gram)
        p_hat = lax.linalg.triangular_solve(lower, left, left_side=False, lower=True, transpose_a=True)
        right = jnp.einsum('gfd,fr->dr', block, p_hat, precision=highest) / N_DP
        approx = jnp.dot(p_hat, right.T, precision=highest)
        fresh = (block - approx[None]).astype(jnp.bfloat16)
        return (p_hat, right, fresh)
    p_all, q_all, fresh_all = lax.map(compress, jnp.arange(EXPERTS, dtype=jnp.int32))
    p_factor = p_all.reshape(EXPERTS * F, R)
    q_factor = jnp.transpose(q_all, (1, 0, 2)).reshape(D, EXPERTS * R)
    new_error = jnp.transpose(fresh_all, (1, 0, 2, 3)).reshape(N_DP * EXPERTS * F, D)
    return (token_grad.reshape(TOKENS, D), p_factor, q_factor, new_error)
```

```python
import jax
import jax.numpy as jnp
from jax import lax
from jax.experimental import pallas as pl
from jax.experimental.pallas import tpu as pltpu
from jax.sharding import Mesh
from jax.sharding import PartitionSpec as P

HIGHEST = lax.Precision.HIGHEST
PIECES = 2


def dot(left, right, dims, precision=None):
    return lax.dot_general(
        left, right, (dims, ((), ())), precision=precision, preferred_element_type=jnp.float32
    )


def swapped(value, axis, mask):
    pairs = [(source, source ^ mask) for source in range(lax.axis_size(axis))]
    return lax.ppermute(value, axis, pairs)


def summed(value):
    bit = 1
    while bit < lax.axis_size("dp"):
        value = value + swapped(value, "dp", bit)
        bit *= 2
    return value + swapped(value, "half", 1)


def basis_kernel(left_ref, out_ref):
    left = left_ref[...]
    rank = left.shape[0]
    gram = lax.dot_general(
        left, left, (((1,), (1,)), ((), ())), precision=HIGHEST, preferred_element_type=jnp.float32
    )
    row_ids = lax.broadcasted_iota(jnp.int32, (rank, rank), 0)
    inverse = jnp.where(
        row_ids == lax.broadcasted_iota(jnp.int32, (rank, rank), 1), 1.0, 0.0
    ).astype(jnp.float32)
    for k in range(rank):
        scale = 1.0 / jnp.sqrt(gram[k : k + 1, k : k + 1])
        gram_row = gram[k : k + 1, :] * scale
        inverse_row = inverse[k : k + 1, :] * scale
        below = jnp.where(row_ids > k, gram[:, k : k + 1] * scale, 0.0)
        gram = gram - below * gram_row
        inverse = jnp.where(row_ids == k, inverse_row, inverse - below * inverse_row)
    out_ref[...] = lax.dot_general(
        inverse, left, (((1,), (0,)), ((), ())), precision=HIGHEST, preferred_element_type=jnp.float32
    )


def basis_of(left_t):
    return pl.pallas_call(
        basis_kernel,
        out_shape=jax.ShapeDtypeStruct(left_t.shape, jnp.float32),
        in_specs=[pl.BlockSpec(memory_space=pltpu.VMEM)],
        out_specs=pl.BlockSpec(memory_space=pltpu.VMEM),
    )(left_t)


def shards(tokens, target, routes, gates, w_gate, w_up, w_down, error, q_start):
    experts = lax.axis_size("expert")
    half = lax.axis_index("half")
    tok, width = tokens.shape
    top = routes.shape[1]
    hidden_half = w_gate.shape[1]
    capacity = max(2, min(tok, 2 * (5 * tok * top // (8 * experts))))
    piece = width // PIECES
    unit = PIECES * capacity
    slots = experts * capacity
    bf16, f32 = jnp.bfloat16, jnp.float32

    def both_halves(mine, other):
        return jnp.where(half == 0, mine, other), jnp.where(half == 0, other, mine)

    own = jnp.concatenate([w_gate, w_up, w_down.T], axis=1)
    first, second = both_halves(own, swapped(own, "half", 1))
    cut = [slice(i * hidden_half, (i + 1) * hidden_half) for i in range(3)]
    packed = jnp.concatenate([part[:, c] for c in cut for part in (first, second)], axis=1)
    weights = lax.all_gather(packed, "dp", axis=0, tiled=True)
    inner = 2 * hidden_half

    expert_ids = jnp.arange(experts, dtype=jnp.int32)
    hits = (routes[:, :, None] == expert_ids).astype(jnp.int32)
    per_token = jnp.sum(hits, axis=1)
    earlier = jnp.cumsum(per_token, axis=0) - per_token
    position = jnp.sum(hits * earlier[:, None, :], axis=2)
    base = (routes * unit + position).T
    places = jnp.arange(PIECES, dtype=jnp.int32)[:, None, None] * capacity + base
    select = (places[..., None] == jnp.arange(experts * unit, dtype=jnp.int32)).astype(bf16)
    spread = jnp.sum(select, axis=1).reshape(PIECES * tok, experts * unit)
    select = select.reshape(PIECES * top * tok, experts * unit)

    def pieces_of(rows):
        return jnp.concatenate(jnp.split(rows, PIECES, axis=-1), axis=0)

    def exchange(rows):
        sent = rows.reshape(experts, unit, piece)
        return lax.all_to_all(sent, "expert", split_axis=0, concat_axis=0, tiled=True)

    def rows_of(received):
        parts = received.reshape(experts, PIECES, capacity, piece)
        return parts.transpose(0, 2, 1, 3).reshape(slots, width)

    def units_of(rows):
        parts = rows.reshape(experts, capacity, PIECES, piece)
        return parts.transpose(0, 2, 1, 3).reshape(experts * unit, piece)

    inbox = rows_of(exchange(dot(spread, pieces_of(tokens), ((0,), (0,))).astype(bf16)))

    q_t = q_start.T
    q_full = jnp.concatenate(both_halves(q_t, swapped(q_t, "half", 1)), axis=0)
    error_left = dot(q_full, error.astype(f32), ((1,), (1,)), HIGHEST)

    pre = dot(inbox, weights[:, : 2 * inner], ((1,), (0,)))
    pre_gate, pre_up = pre[:, :inner], pre[:, inner:]
    sig = jax.nn.sigmoid(pre_gate)
    act = pre_gate * sig
    hidden = (act * pre_up).astype(bf16)
    down = weights[:, 2 * inner :]
    expert_out = dot(hidden, down, ((1,), (1,))).astype(bf16)
    returned = exchange(units_of(expert_out)).reshape(experts * unit, piece)
    picked = dot(select, returned, ((1,), (0,))).reshape(PIECES, top, tok, piece)
    gate = gates.T[None, :, :, None]
    layer_sum = jnp.sum(gate * picked, axis=1)
    slope = layer_sum - pieces_of(target).reshape(PIECES, tok, piece).astype(f32)
    out_grad = (gate * slope[:, None]).astype(bf16).reshape(PIECES * top * tok, piece)
    grad_in = rows_of(exchange(dot(select, out_grad, ((0,), (0,))).astype(bf16)))

    hidden_parts = (hidden[:, :hidden_half], hidden[:, hidden_half:])
    hidden_mine, hidden_theirs = both_halves(*hidden_parts)
    hidden_other = swapped(hidden_theirs, "half", 1)
    grad_other = swapped(grad_in, "half", 1)

    hidden_grad = dot(grad_in, down, ((1,), (0,)))
    gate_grad = (hidden_grad * pre_up * sig * (1.0 + pre_gate * (1.0 - sig))).astype(bf16)
    up_grad = (hidden_grad * act).astype(bf16)
    both_grads = jnp.concatenate([gate_grad, up_grad], axis=1)
    token_part = dot(both_grads, weights[:, : 2 * inner], ((1,), (1,))).astype(bf16)
    slot_grad = exchange(units_of(token_part)).reshape(experts * unit, piece)
    token_grad = dot(spread, slot_grad, ((1,), (0,))).astype(bf16)
    token_grad = jnp.concatenate(jnp.split(token_grad, PIECES, axis=0), axis=1)

    grad_q = dot(q_full, grad_in.astype(f32), ((1,), (1,)), HIGHEST)
    zeros = jnp.zeros_like(error_left)
    left = dot(grad_q, hidden.astype(f32), ((1,), (0,)), HIGHEST) + jnp.concatenate(
        both_halves(error_left, zeros), axis=1
    )
    basis = basis_of(summed(left))
    basis_mine = jnp.where(half == 0, basis[:, :hidden_half], basis[:, hidden_half:])

    hidden_basis = dot(basis, hidden.astype(f32), ((1,), (1,)), HIGHEST)
    right = dot(hidden_basis, grad_in.astype(f32), ((1,), (0,)), HIGHEST) + dot(
        basis_mine, error.astype(f32), ((1,), (0,)), HIGHEST
    )
    right = summed(right) / lax.axis_size("dp")
    rank_half = right.shape[0] // 2
    q_columns = jnp.where(half == 0, right[:rank_half], right[rank_half:])
    q_rows = width // lax.axis_size("dp")
    q_factor = lax.dynamic_slice_in_dim(q_columns, lax.axis_index("dp") * q_rows, q_rows, 1).T

    merged = (
        dot(hidden_mine, grad_in, ((0,), (0,)))
        + dot(hidden_other, grad_other, ((0,), (0,)))
        + error.astype(f32)
    )
    new_error = (merged - dot(basis_mine, right, ((0,), (0,)), HIGHEST)).astype(bf16)
    return token_grad, basis_mine.T, q_factor, new_error


def solution(mesh):
    experts = mesh.shape["expert"] // 2
    split = Mesh(
        mesh.devices.reshape(mesh.shape["dp"], experts, 2), ("dp", "expert", "half")
    )
    pair = ("expert", "half")
    rows = P(("dp",) + pair, None)
    in_specs = (rows, rows, rows, rows, P("dp", pair), P("dp", pair), P(pair, "dp"), rows, P(None, pair))
    out_specs = (rows, P(pair, None), P("dp", pair), rows)
    return jax.shard_map(shards, mesh=split, in_specs=in_specs, out_specs=out_specs, check_vma=False)
```

```python
import jax
import jax.numpy as jnp
from jax import lax
from jax.experimental import pallas as pl
from jax.experimental.pallas import tpu as pltpu
from jax.sharding import Mesh
from jax.sharding import PartitionSpec as P

HIGHEST = lax.Precision.HIGHEST
BF16, F32 = jnp.bfloat16, jnp.float32
PIECES = 2
BLOCK = 4
NN = ((1,), (0,))
NT = ((1,), (1,))
TN = ((0,), (0,))
DP = ("group", "core")
PLANE = ("group", "half")


def dot(left, right, dims, precision=None):
    return lax.dot_general(
        left, right, (dims, ((), ())), precision=precision, preferred_element_type=F32
    )


def thirds(value):
    high = value.astype(BF16)
    rest = value - high.astype(F32)
    middle = rest.astype(BF16)
    low = (rest - middle.astype(F32)).astype(BF16)
    return jnp.concatenate([high, middle, low], axis=0)


def folded(value):
    rows = value.shape[0] // 3
    return value[:rows] + value[rows : 2 * rows] + value[2 * rows :]


def local_call(kernel, outs, scratch, *operands, hbm=(), out_hbm=(), memory=16, smem=()):
    def specs(count, there, scalars=()):
        spaces = [pltpu.HBM if i in there else pltpu.VMEM for i in range(count)]
        spaces = [pltpu.SMEM if i in scalars else space for i, space in enumerate(spaces)]
        return [pl.BlockSpec(memory_space=space) for space in spaces]

    return pl.pallas_call(
        kernel,
        out_shape=[jax.ShapeDtypeStruct(shape, dtype) for shape, dtype in outs],
        in_specs=specs(len(operands), hbm, smem),
        out_specs=specs(len(outs), out_hbm),
        scratch_shapes=scratch,
        compiler_params=pltpu.CompilerParams(vmem_limit_bytes=memory * 2**20),
    )(*operands)


def sides_of(array, width):
    return [array.at[:, pl.ds(side * width, width)] for side in range(2)]


def blocks_of(array, rows):
    return [array.at[pl.ds(i * rows, rows), :] for i in range(array.shape[0] // rows)]


def copies_of(sources, targets, sems, first):
    return [
        pltpu.make_async_copy(source, target, sems.at[first + i])
        for i, (source, target) in enumerate(zip(sources, targets))
    ]


def started(copies):
    for copy in copies:
        copy.start()


def finished(copies):
    for copy in copies:
        copy.wait()


def weight_copies(w_ref, proj_ref, down_ref, sems, half):
    proj, down = [], []
    for side in range(2):
        start = side * 3 * half
        proj.append(w_ref.at[:, pl.ds(start, 2 * half)])
        down.append(w_ref.at[:, pl.ds(start + 2 * half, half)])
    return (
        copies_of(proj, [proj_ref.at[side] for side in range(2)], sems, 0),
        copies_of(down, [down_ref.at[side] for side in range(2)], sems, 2),
    )


def to_rows(units_ref, gather_ref, rows_ref, arrivals):
    count, piece = gather_ref.shape[0], units_ref.shape[1]
    part = count // PIECES
    for i, copy in enumerate(arrivals):
        copy.wait()
        block = dot(gather_ref[...], units_ref[i * count : (i + 1) * count, :], NN).astype(BF16)
        for j in range(PIECES):
            rows_ref[i * part : (i + 1) * part, j * piece : (j + 1) * piece] = block[
                j * part : (j + 1) * part
            ]


def to_units(rows_ref, scatter_ref, units_ref, departures):
    count, piece = scatter_ref.shape[0], units_ref.shape[1]
    part = count // PIECES
    for i, copy in enumerate(departures):
        block = jnp.concatenate(
            [
                rows_ref[i * part : (i + 1) * part, j * piece : (j + 1) * piece]
                for j in range(PIECES)
            ],
            axis=0,
        )
        units_ref[i * count : (i + 1) * count, :] = dot(scatter_ref[...], block, NN).astype(BF16)
        copy.start()


def forward_kernel(
    got_hbm, gather_ref, scatter_ref, w_hbm, units_hbm, hidden_ref, act_hbm, slope_hbm,
    proj_ref, down_ref, got_ref, rows_ref, outs_ref, units_ref, act_ref, slope_ref, sems,
):
    half = hidden_ref.shape[1] // 2
    piece = got_ref.shape[1]
    count = gather_ref.shape[0]
    blocks = got_ref.shape[0] // count
    arrivals = copies_of(blocks_of(got_hbm, count), blocks_of(got_ref, count), sems, 8)
    departures = copies_of(
        blocks_of(units_ref, count), blocks_of(units_hbm, count), sems, 8 + blocks
    )
    proj, down = weight_copies(w_hbm, proj_ref, down_ref, sems, half)
    kept = copies_of(sides_of(act_ref, half), sides_of(act_hbm, half), sems, 4)
    kept += copies_of(sides_of(slope_ref, half), sides_of(slope_hbm, half), sems, 6)
    started(arrivals + proj + down)
    to_rows(got_ref, gather_ref, rows_ref, arrivals)
    rows = rows_ref[...]
    for side in range(2):
        proj[side].wait()
        pre = dot(rows, proj_ref[side], NN)
        pre_gate, pre_up = pre[:, :half], pre[:, half:]
        sig = jax.nn.sigmoid(pre_gate)
        act = pre_gate * sig
        columns = slice(side * half, (side + 1) * half)
        hidden_ref[:, columns] = (act * pre_up).astype(BF16)
        act_ref[:, columns] = act
        slope_ref[:, columns] = pre_up * sig * (1.0 + pre_gate * (1.0 - sig))
        kept[side].start()
        kept[2 + side].start()
    finished(down)
    for j in range(PIECES):
        cols = slice(j * piece, (j + 1) * piece)
        out = dot(hidden_ref[:, :half], down_ref[0, cols, :], NT)
        out = out + dot(hidden_ref[:, half:], down_ref[1, cols, :], NT)
        outs_ref[:, cols] = out.astype(BF16)
    to_units(outs_ref, scatter_ref, units_ref, departures)
    finished(kept + departures)


def backward_kernel(
    got_hbm, act_hbm, slope_hbm, hidden_ref, q_ref, error_left_ref, gather_ref, scatter_ref, w_hbm,
    units_hbm, rows_hbm, left_ref,
    proj_ref, down_ref, got_ref, rows_ref, outs_ref, units_ref, act_ref, slope_ref, sems, grads_ref,
):
    half = act_ref.shape[1] // 2
    piece = units_ref.shape[1]
    count = gather_ref.shape[0]
    blocks = got_ref.shape[0] // count
    arrivals = copies_of(blocks_of(got_hbm, count), blocks_of(got_ref, count), sems, 8)
    departures = copies_of(
        blocks_of(units_ref, count), blocks_of(units_hbm, count), sems, 8 + blocks
    )
    proj, down = weight_copies(w_hbm, proj_ref, down_ref, sems, half)
    kept = copies_of(sides_of(act_hbm, half), sides_of(act_ref, half), sems, 4)
    kept += copies_of(sides_of(slope_hbm, half), sides_of(slope_ref, half), sems, 6)
    out_rows = copies_of([rows_ref], [rows_hbm], sems, 8 + 2 * blocks)
    started(arrivals + down + kept + proj)
    to_rows(got_ref, gather_ref, rows_ref, arrivals)
    started(out_rows)
    rows = rows_ref[...]
    grad_q = folded(dot(thirds(q_ref[...]), rows, NT))
    left = folded(dot(thirds(grad_q), hidden_ref[...], NN))
    left_ref[:, :half] = left[:, :half] + error_left_ref[...]
    left_ref[:, half:] = left[:, half:]
    for side in range(2):
        columns = slice(side * half, (side + 1) * half)
        down[side].wait()
        hidden_grad = dot(rows, down_ref[side], NN)
        kept[side].wait()
        kept[2 + side].wait()
        grads_ref[side, :, :half] = (hidden_grad * slope_ref[:, columns]).astype(BF16)
        grads_ref[side, :, half:] = (hidden_grad * act_ref[:, columns]).astype(BF16)
    finished(proj)
    for j in range(PIECES):
        cols = slice(j * piece, (j + 1) * piece)
        out = dot(grads_ref[0], proj_ref[0, cols, :], NT)
        out = out + dot(grads_ref[1], proj_ref[1, cols, :], NT)
        outs_ref[:, cols] = out.astype(BF16)
    to_units(outs_ref, scatter_ref, units_ref, departures)
    finished(departures + out_rows)


def basis_kernel(
    core_ref, left_ref, hidden_ref, rows_hbm, error_hbm, basis_ref, terms_ref, right_ref, away_ref,
    rows_ref, error_ref, sems,
):
    copies = copies_of([rows_hbm, error_hbm], [rows_ref, error_ref], sems, 0)
    started(copies)
    left = left_ref[...]
    rank = left.shape[0]
    half = left.shape[1] // 2
    gram = dot(left, left, NT, HIGHEST)
    row_ids = lax.broadcasted_iota(jnp.int32, (rank, rank), 0)
    inverse = jnp.where(
        row_ids == lax.broadcasted_iota(jnp.int32, (rank, rank), 1), 1.0, 0.0
    ).astype(F32)
    for k in range(rank):
        scale = 1.0 / jnp.sqrt(gram[k : k + 1, k : k + 1])
        gram_row = gram[k : k + 1, :] * scale
        inverse_row = inverse[k : k + 1, :] * scale
        below = jnp.where(row_ids > k, gram[:, k : k + 1] * scale, 0.0)
        gram = gram - below * gram_row
        inverse = jnp.where(row_ids == k, inverse_row, inverse - below * inverse_row)
    basis = dot(inverse, left, NN, HIGHEST)
    mine = basis[:, :half]
    basis_ref[...] = mine
    terms = thirds(mine)
    terms_ref[...] = jnp.concatenate(
        [terms[:rank], terms[:rank], terms[rank : 2 * rank], terms[rank : 2 * rank]], axis=0
    )
    finished(copies)
    hidden_basis = folded(dot(thirds(basis), hidden_ref[...], NT))
    right = folded(dot(terms, error_ref[...], NN))
    right = right + folded(dot(thirds(hidden_basis), rows_ref[...], NN))
    span = right_ref.shape[1]
    first = core_ref[0] == 0
    right_ref[...] = jnp.where(first, right[:, :span], right[:, span:])
    away_ref[...] = jnp.where(first, right[:, span:], right[:, :span])


def error_kernel(merged_ref, terms_ref, right_ref, fresh_ref):
    right = right_ref[...]
    rank = right.shape[0]
    parts = thirds(right)
    high, middle = parts[:rank], parts[rank : 2 * rank]
    approx = dot(terms_ref[...], jnp.concatenate([high, middle, high, middle], axis=0), TN)
    fresh_ref[...] = (merged_ref[...] - approx).astype(BF16)


def moved(value, mask):
    count = lax.axis_size("group") * lax.axis_size("half")
    return lax.ppermute(value, PLANE, [(source, source ^ mask) for source in range(count)])


def plane_sum(value, flip):
    near, far, both = moved(value, 2), moved(value, 4), moved(value, 6)
    value = (value + near) + (far + both)
    near, far, both = moved(value, 8), moved(value, 1), moved(value, 9)
    return (value + near) + flip(far + both)


def shards(tokens, target, routes, gates, w_gate, w_up, w_down, error, q_start):
    experts = lax.axis_size("expert")
    half = lax.axis_index("half")
    tok, width = tokens.shape
    top = routes.shape[1]
    hidden_half = w_gate.shape[1]
    inner = 2 * hidden_half
    capacity = max(2, min(tok, 2 * (5 * tok * top // (8 * experts))))
    piece = width // PIECES
    unit = PIECES * capacity
    slots = experts * capacity
    rank = 2 * q_start.shape[1]

    own = jnp.concatenate([w_gate, w_up, w_down.T], axis=1)
    packed = jnp.concatenate([own, moved(own, 1)], axis=1)

    expert_ids = jnp.arange(experts, dtype=jnp.int32)
    hits = (routes[:, :, None] == expert_ids).astype(jnp.int32)
    per_token = jnp.sum(hits, axis=1)
    earlier = jnp.cumsum(per_token, axis=0) - per_token
    position = jnp.sum(hits * earlier[:, None, :], axis=2)
    base = (routes * unit + position).T
    lanes = jnp.arange(experts * unit, dtype=jnp.int32)
    places = jnp.arange(PIECES, dtype=jnp.int32)[:, None, None] * capacity + base
    select = (places[..., None] == lanes).astype(BF16)
    spread = jnp.sum(select, axis=1).reshape(PIECES * tok, experts * unit)
    select = select.reshape(PIECES * top * tok, experts * unit)

    block = min(BLOCK, experts)
    order = (
        jnp.arange(PIECES, dtype=jnp.int32)[:, None, None] * capacity
        + jnp.arange(block, dtype=jnp.int32)[None, :, None] * unit
        + jnp.arange(capacity, dtype=jnp.int32)[None, None, :]
    ).reshape(block * unit)
    block_lanes = jnp.arange(block * unit, dtype=jnp.int32)
    gather = (order[:, None] == block_lanes).astype(BF16)
    scatter = (block_lanes[:, None] == order).astype(BF16)

    def pieces_of(rows):
        return jnp.concatenate(jnp.split(rows, PIECES, axis=-1), axis=0)

    def exchange(rows):
        sent = rows.reshape(experts, unit, piece)
        back = lax.all_to_all(sent, "expert", split_axis=0, concat_axis=0, tiled=True)
        return back.reshape(experts * unit, piece)

    send = dot(spread, pieces_of(tokens), TN).astype(BF16)
    packed, send = lax.optimization_barrier((packed, send))
    weights = lax.all_gather(packed, DP, axis=0, tiled=True)
    inbox = exchange(send)

    q_mine = q_start.T
    q_other = moved(q_mine, 1)
    q_full = jnp.concatenate(
        [jnp.where(half == 0, q_mine, q_other), jnp.where(half == 0, q_other, q_mine)], axis=0
    )
    error_left = dot(q_full, error.astype(F32), NT, HIGHEST)
    inbox, q_full, error_left = lax.optimization_barrier((inbox, q_full, error_left))

    unit_shape, row_shape = (experts * unit, piece), (slots, width)
    blocks = experts // block
    scratch = [
        pltpu.VMEM((2, width, inner), BF16),
        pltpu.VMEM((2, width, hidden_half), BF16),
        pltpu.VMEM(unit_shape, BF16),
        pltpu.VMEM(row_shape, BF16),
        pltpu.VMEM(row_shape, BF16),
        pltpu.VMEM(unit_shape, BF16),
        pltpu.VMEM((slots, inner), F32),
        pltpu.VMEM((slots, inner), F32),
        pltpu.SemaphoreType.DMA((9 + 2 * blocks,)),
    ]
    returned, hidden, act, act_slope = local_call(
        forward_kernel,
        [(unit_shape, BF16), ((slots, inner), BF16), ((slots, inner), F32), ((slots, inner), F32)],
        scratch,
        inbox, gather, scatter, weights, hbm=(0, 3), out_hbm=(0, 2, 3), memory=58,
    )
    returned = exchange(returned)
    picked = dot(select, returned, NN).reshape(PIECES, top, tok, piece)
    gate = gates.T[None, :, :, None]
    layer_sum = jnp.sum(gate * picked, axis=1)
    slope = layer_sum - pieces_of(target).reshape(PIECES, tok, piece).astype(F32)
    out_grad = (gate * slope[:, None]).astype(BF16).reshape(PIECES * top * tok, piece)
    grad_got = exchange(dot(select, out_grad, TN).astype(BF16))
    hidden_other = moved(hidden[:, hidden_half:], 1)
    grad_got, hidden_other = lax.optimization_barrier((grad_got, hidden_other))

    token_part, rows, left = local_call(
        backward_kernel,
        [(unit_shape, BF16), (row_shape, BF16), ((rank, inner), F32)],
        scratch + [pltpu.VMEM((2, slots, inner), BF16)],
        grad_got, act, act_slope, hidden, q_full, error_left, gather, scatter, weights,
        hbm=(0, 1, 2, 8), out_hbm=(0, 1), memory=58,
    )
    slot_grad = exchange(token_part)
    token_grad = dot(spread, slot_grad, NN).astype(BF16)
    token_grad = jnp.concatenate(jnp.split(token_grad, PIECES, axis=0), axis=1)

    def flip(value):
        return jnp.concatenate([value[:, hidden_half:], value[:, :hidden_half]], axis=1)

    left = jnp.sum(lax.all_gather(left, "core"), axis=0)
    left, sent_rows = lax.optimization_barrier((left, rows))
    rows_other = moved(sent_rows, 1)
    left, rows_other = lax.optimization_barrier((plane_sum(left, flip), rows_other))
    core = lax.axis_index("core")
    span = width // lax.axis_size("core")
    basis, terms, right, right_away = local_call(
        basis_kernel,
        [
            ((rank, hidden_half), F32),
            ((4 * rank, hidden_half), BF16),
            ((rank, span), F32),
            ((rank, span), F32),
        ],
        [
            pltpu.VMEM(row_shape, BF16),
            pltpu.VMEM((hidden_half, width), BF16),
            pltpu.SemaphoreType.DMA((2,)),
        ],
        core.reshape(1), left, hidden, rows, error, hbm=(3, 4), smem=(0,),
    )
    merged = (
        dot(hidden[:, :hidden_half], rows, TN)
        + dot(hidden_other, rows_other, TN)
        + error.astype(F32)
    )
    right = right + lax.ppermute(right_away, "core", [(0, 1), (1, 0)])
    right = plane_sum(right, lambda value: value) / (lax.axis_size("group") * lax.axis_size("core"))
    right = lax.all_gather(right, "core", axis=1, tiled=True)
    (new_error,) = local_call(
        error_kernel, [((hidden_half, width), BF16)], [], merged, terms, right
    )
    q_columns = jnp.where(half == 0, right[: rank // 2], right[rank // 2 :])
    replicas = lax.axis_size("group") * lax.axis_size("core")
    replica = lax.axis_index("group") * lax.axis_size("core") + lax.axis_index("core")
    q_rows = width // replicas
    q_factor = lax.dynamic_slice_in_dim(q_columns, replica * q_rows, q_rows, 1).T
    return token_grad, basis.T, q_factor, new_error


def solution(mesh):
    replicas, places = mesh.shape["dp"], mesh.shape["expert"]
    split = Mesh(
        mesh.devices.reshape(replicas // 2, 2, places // 2, 2),
        ("group", "core", "expert", "half"),
    )
    pair = ("expert", "half")
    rows = P(DP + pair, None)
    in_specs = (rows, rows, rows, rows, P(DP, pair), P(DP, pair), P(pair, DP), rows, P(None, pair))
    out_specs = (rows, P(pair, None), P(DP, pair), rows)
    return jax.shard_map(shards, mesh=split, in_specs=in_specs, out_specs=out_specs, check_vma=False)
```

```python
import functools

import jax
import jax.numpy as jnp
from jax import lax
from jax.experimental import pallas as pl
from jax.experimental.pallas import tpu as pltpu
from jax.sharding import Mesh
from jax.sharding import PartitionSpec as P

HIGHEST = lax.Precision.HIGHEST
BF16, F32 = jnp.bfloat16, jnp.float32
PIECES = 2
BLOCK = 4
NN = ((1,), (0,))
NT = ((1,), (1,))
TN = ((0,), (0,))
DP = ("along", "across", "core")
PLANE = ("along", "across", "half")


def dot(left, right, dims, precision=None):
    return lax.dot_general(
        left, right, (dims, ((), ())), precision=precision, preferred_element_type=F32
    )


def thirds(value):
    high = value.astype(BF16)
    rest = value - high.astype(F32)
    middle = rest.astype(BF16)
    low = (rest - middle.astype(F32)).astype(BF16)
    return jnp.concatenate([high, middle, low], axis=0)


def folded(value):
    rows = value.shape[0] // 3
    return value[:rows] + value[rows : 2 * rows] + value[2 * rows :]


def local_call(kernel, outs, scratch, *operands, hbm=(), out_hbm=(), memory=16, smem=()):
    def specs(count, there, scalars=()):
        spaces = [pltpu.HBM if i in there else pltpu.VMEM for i in range(count)]
        spaces = [pltpu.SMEM if i in scalars else space for i, space in enumerate(spaces)]
        return [pl.BlockSpec(memory_space=space) for space in spaces]

    return pl.pallas_call(
        kernel,
        out_shape=[jax.ShapeDtypeStruct(shape, dtype) for shape, dtype in outs],
        in_specs=specs(len(operands), hbm, smem),
        out_specs=specs(len(outs), out_hbm),
        scratch_shapes=scratch,
        compiler_params=pltpu.CompilerParams(vmem_limit_bytes=memory * 2**20),
    )(*operands)


def sides_of(array, width):
    return [array.at[:, pl.ds(side * width, width)] for side in range(2)]


def blocks_of(array, rows):
    return [array.at[pl.ds(i * rows, rows), :] for i in range(array.shape[0] // rows)]


def copies_of(sources, targets, sems, first):
    return [
        pltpu.make_async_copy(source, target, sems.at[first + i])
        for i, (source, target) in enumerate(zip(sources, targets))
    ]


def started(copies):
    for copy in copies:
        copy.start()


def finished(copies):
    for copy in copies:
        copy.wait()


def weight_copies(w_ref, proj_ref, down_ref, sems, half):
    proj, down = [], []
    for side in range(2):
        start = side * 3 * half
        proj.append(w_ref.at[:, pl.ds(start, 2 * half)])
        down.append(w_ref.at[:, pl.ds(start + 2 * half, half)])
    return (
        copies_of(proj, [proj_ref.at[side] for side in range(2)], sems, 0),
        copies_of(down, [down_ref.at[side] for side in range(2)], sems, 2),
    )


def reorder(count, capacity, dim):
    rows = lax.broadcasted_iota(jnp.int32, (count, count), dim)
    part = count // PIECES
    pieces = sum((rows >= part * j).astype(jnp.int32) for j in range(1, PIECES))
    inside = rows - part * pieces
    experts = sum(
        (inside >= capacity * i).astype(jnp.int32) for i in range(1, part // capacity)
    )
    place = inside - capacity * experts + capacity * pieces + PIECES * capacity * experts
    return (place == lax.broadcasted_iota(jnp.int32, (count, count), 1 - dim)).astype(BF16)


def to_rows(units_ref, rows_ref, arrivals, capacity):
    piece = units_ref.shape[1]
    count = units_ref.shape[0] // len(arrivals)
    part = count // PIECES
    order = reorder(count, capacity, 0)
    for i, copy in enumerate(arrivals):
        copy.wait()
        block = dot(order, units_ref[i * count : (i + 1) * count, :], NN).astype(BF16)
        for j in range(PIECES):
            rows_ref[i * part : (i + 1) * part, j * piece : (j + 1) * piece] = block[
                j * part : (j + 1) * part
            ]


def to_units(rows_ref, units_ref, departures, capacity):
    piece = units_ref.shape[1]
    count = units_ref.shape[0] // len(departures)
    part = count // PIECES
    order = reorder(count, capacity, 1)
    for i, copy in enumerate(departures):
        block = jnp.concatenate(
            [
                rows_ref[i * part : (i + 1) * part, j * piece : (j + 1) * piece]
                for j in range(PIECES)
            ],
            axis=0,
        )
        units_ref[i * count : (i + 1) * count, :] = dot(order, block, NN).astype(BF16)
        copy.start()


def forward_kernel(
    blocks, capacity, got_hbm, w_hbm, units_hbm, hidden_hbm, act_hbm, slope_hbm,
    proj_ref, down_ref, got_ref, rows_ref, outs_ref, units_ref, act_ref, slope_ref, hidden_ref, sems,
):
    half = hidden_ref.shape[1] // 2
    piece = got_ref.shape[1]
    count = got_ref.shape[0] // blocks
    arrivals = copies_of(blocks_of(got_hbm, count), blocks_of(got_ref, count), sems, 12)
    departures = copies_of(
        blocks_of(units_ref, count), blocks_of(units_hbm, count), sems, 12 + blocks
    )
    proj, down = weight_copies(w_hbm, proj_ref, down_ref, sems, half)
    kept = copies_of(sides_of(act_ref, half), sides_of(act_hbm, half), sems, 4)
    kept += copies_of(sides_of(slope_ref, half), sides_of(slope_hbm, half), sems, 6)
    kept += copies_of(sides_of(hidden_ref, half), sides_of(hidden_hbm, half), sems, 8)
    started(arrivals + proj + down)
    to_rows(got_ref, rows_ref, arrivals, capacity)
    rows = rows_ref[...]
    for side in range(2):
        proj[side].wait()
        pre = dot(rows, proj_ref[side], NN)
        pre_gate, pre_up = pre[:, :half], pre[:, half:]
        sig = jax.nn.sigmoid(pre_gate)
        act = pre_gate * sig
        columns = slice(side * half, (side + 1) * half)
        hidden_ref[:, columns] = (act * pre_up).astype(BF16)
        act_ref[:, columns] = act
        slope_ref[:, columns] = pre_up * sig * (1.0 + pre_gate * (1.0 - sig))
        started(kept[side::2])
    finished(down)
    for j in range(PIECES):
        cols = slice(j * piece, (j + 1) * piece)
        out = dot(hidden_ref[:, :half], down_ref[0, cols, :], NT)
        out = out + dot(hidden_ref[:, half:], down_ref[1, cols, :], NT)
        outs_ref[:, cols] = out.astype(BF16)
    to_units(outs_ref, units_ref, departures, capacity)
    finished(kept + departures)


def backward_kernel(
    blocks, capacity, got_hbm, act_hbm, slope_hbm, hidden_hbm, q_hbm, error_left_hbm, w_hbm,
    units_hbm, rows_hbm, left_hbm,
    proj_ref, down_ref, got_ref, rows_ref, outs_ref, units_ref, act_ref, slope_ref, hidden_ref, sems,
    grads_ref, q_ref, error_left_ref, left_ref,
):
    half = act_ref.shape[1] // 2
    piece = units_ref.shape[1]
    count = got_ref.shape[0] // blocks
    arrivals = copies_of(blocks_of(got_hbm, count), blocks_of(got_ref, count), sems, 12)
    departures = copies_of(
        blocks_of(units_ref, count), blocks_of(units_hbm, count), sems, 12 + blocks
    )
    proj, down = weight_copies(w_hbm, proj_ref, down_ref, sems, half)
    kept = copies_of(sides_of(act_hbm, half), sides_of(act_ref, half), sems, 4)
    kept += copies_of(sides_of(slope_hbm, half), sides_of(slope_ref, half), sems, 6)
    small = copies_of([q_hbm, hidden_hbm], [q_ref, hidden_ref], sems, 8)
    small += copies_of([error_left_hbm], [error_left_ref], sems, 10)
    out_rows = copies_of([rows_ref], [rows_hbm], sems, 12 + 2 * blocks)
    out_left = copies_of([left_ref], [left_hbm], sems, 11)
    started(arrivals + small + down + kept + proj)
    to_rows(got_ref, rows_ref, arrivals, capacity)
    started(out_rows)
    rows = rows_ref[...]
    finished(small)
    grad_q = folded(dot(thirds(q_ref[...]), rows, NT))
    left = folded(dot(thirds(grad_q), hidden_ref[...], NN))
    left_ref[:, :half] = left[:, :half] + error_left_ref[...]
    left_ref[:, half:] = left[:, half:]
    started(out_left)
    for side in range(2):
        columns = slice(side * half, (side + 1) * half)
        down[side].wait()
        hidden_grad = dot(rows, down_ref[side], NN)
        kept[side].wait()
        kept[2 + side].wait()
        grads_ref[side, :, :half] = (hidden_grad * slope_ref[:, columns]).astype(BF16)
        grads_ref[side, :, half:] = (hidden_grad * act_ref[:, columns]).astype(BF16)
    finished(proj)
    for j in range(PIECES):
        cols = slice(j * piece, (j + 1) * piece)
        out = dot(grads_ref[0], proj_ref[0, cols, :], NT)
        out = out + dot(grads_ref[1], proj_ref[1, cols, :], NT)
        outs_ref[:, cols] = out.astype(BF16)
    to_units(outs_ref, units_ref, departures, capacity)
    finished(departures + out_rows + out_left)


def basis_kernel(
    core_ref, left_ref, hidden_ref, rows_hbm, error_hbm, basis_ref, right_ref, away_ref,
    rows_ref, error_ref, sems,
):
    copies = copies_of([rows_hbm, error_hbm], [rows_ref, error_ref], sems, 0)
    started(copies)
    left = left_ref[...]
    rank = left.shape[0]
    half = left.shape[1] // 2
    gram = dot(left, left, NT, HIGHEST)
    row_ids = lax.broadcasted_iota(jnp.int32, (rank, rank), 0)
    inverse = jnp.where(
        row_ids == lax.broadcasted_iota(jnp.int32, (rank, rank), 1), 1.0, 0.0
    ).astype(F32)
    for k in range(rank):
        scale = 1.0 / jnp.sqrt(gram[k : k + 1, k : k + 1])
        gram_row = gram[k : k + 1, :] * scale
        inverse_row = inverse[k : k + 1, :] * scale
        below = jnp.where(row_ids > k, gram[:, k : k + 1] * scale, 0.0)
        gram = gram - below * gram_row
        inverse = jnp.where(row_ids == k, inverse_row, inverse - below * inverse_row)
    basis = dot(inverse, left, NN, HIGHEST)
    mine = basis[:, :half]
    basis_ref[...] = mine
    terms = thirds(mine)
    finished(copies)
    hidden_basis = folded(dot(thirds(basis), hidden_ref[...], NT))
    right = folded(dot(terms, error_ref[...], NN))
    right = right + folded(dot(thirds(hidden_basis), rows_ref[...], NN))
    span = right_ref.shape[1]
    first = core_ref[0] == 0
    right_ref[...] = jnp.where(first, right[:, :span], right[:, span:])
    away_ref[...] = jnp.where(first, right[:, span:], right[:, :span])


def error_kernel(merged_ref, basis_ref, right_ref, fresh_ref):
    rank = right_ref.shape[0]
    basis, right = thirds(basis_ref[...]), thirds(right_ref[...])
    high, middle = right[:rank], right[rank : 2 * rank]
    left = jnp.concatenate([basis[:rank], basis[:rank], basis[rank : 2 * rank]], axis=0)
    approx = dot(left, jnp.concatenate([high, middle, high], axis=0), TN)
    fresh_ref[...] = (merged_ref[...] - approx).astype(BF16)


def moved(value, mask):
    count = lax.axis_size("along") * lax.axis_size("across") * lax.axis_size("half")
    return lax.ppermute(value, PLANE, [(source, source ^ mask) for source in range(count)])


def pairs_sum(values):
    while values.shape[0] > 1:
        half = values.shape[0] // 2
        values = values[:half] + values[half:]
    return values[0]


def shards(tokens, target, routes, gates, w_gate, w_up, w_down, error, q_start):
    experts = lax.axis_size("expert")
    half = lax.axis_index("half")
    tok, width = tokens.shape
    top = routes.shape[1]
    hidden_half = w_gate.shape[1]
    inner = 2 * hidden_half
    capacity = max(2, min(tok, 2 * (5 * tok * top // (8 * experts))))
    piece = width // PIECES
    unit = PIECES * capacity
    slots = experts * capacity
    rank = 2 * q_start.shape[1]

    own = jnp.concatenate([w_gate, w_up, w_down.T], axis=1)
    packed = jnp.concatenate([own, moved(own, 1)], axis=1)

    expert_ids = jnp.arange(experts, dtype=jnp.int32)
    hits = (routes[:, :, None] == expert_ids).astype(jnp.int32)
    per_token = jnp.sum(hits, axis=1)
    earlier = jnp.cumsum(per_token, axis=0) - per_token
    position = jnp.sum(hits * earlier[:, None, :], axis=2)
    base = (routes * unit + position).T
    lanes = jnp.arange(experts * unit, dtype=jnp.int32)
    places = jnp.arange(PIECES, dtype=jnp.int32)[:, None, None] * capacity + base
    select = (places[..., None] == lanes).astype(BF16)
    spread = jnp.sum(select, axis=1).reshape(PIECES * tok, experts * unit)
    select = select.reshape(PIECES * top * tok, experts * unit)

    def pieces_of(rows):
        return jnp.concatenate(jnp.split(rows, PIECES, axis=-1), axis=0)

    def exchange(rows):
        sent = rows.reshape(experts, unit, piece)
        back = lax.all_to_all(sent, "expert", split_axis=0, concat_axis=0, tiled=True)
        return back.reshape(experts * unit, piece)

    send = dot(spread, pieces_of(tokens), TN).astype(BF16)
    packed, send = lax.optimization_barrier((packed, send))
    weights = lax.all_gather(packed, DP, axis=0, tiled=True)
    inbox = exchange(send)

    q_mine = q_start.T
    q_other = moved(q_mine, 1)
    q_full = jnp.concatenate(
        [jnp.where(half == 0, q_mine, q_other), jnp.where(half == 0, q_other, q_mine)], axis=0
    )
    error_left = dot(q_full, error.astype(F32), NT, HIGHEST)
    inbox, q_full, error_left = lax.optimization_barrier((inbox, q_full, error_left))

    unit_shape, row_shape = (experts * unit, piece), (slots, width)
    blocks = experts // min(BLOCK, experts)
    scratch = [
        pltpu.VMEM((2, width, inner), BF16),
        pltpu.VMEM((2, width, hidden_half), BF16),
        pltpu.VMEM(unit_shape, BF16),
        pltpu.VMEM(row_shape, BF16),
        pltpu.VMEM(row_shape, BF16),
        pltpu.VMEM(unit_shape, BF16),
        pltpu.VMEM((slots, inner), F32),
        pltpu.VMEM((slots, inner), F32),
        pltpu.VMEM((slots, inner), BF16),
        pltpu.SemaphoreType.DMA((13 + 2 * blocks,)),
    ]
    returned, hidden, act, act_slope = local_call(
        functools.partial(forward_kernel, blocks, capacity),
        [(unit_shape, BF16), ((slots, inner), BF16), ((slots, inner), F32), ((slots, inner), F32)],
        scratch,
        inbox, weights, hbm=(0, 1), out_hbm=(0, 1, 2, 3), memory=58,
    )
    returned = exchange(returned)
    picked = dot(select, returned, NN).reshape(PIECES, top, tok, piece)
    gate = gates.T[None, :, :, None]
    layer_sum = jnp.sum(gate * picked, axis=1)
    slope = layer_sum - pieces_of(target).reshape(PIECES, tok, piece).astype(F32)
    out_grad = (gate * slope[:, None]).astype(BF16).reshape(PIECES * top * tok, piece)
    grad_got = exchange(dot(select, out_grad, TN).astype(BF16))
    hidden_other = moved(hidden[:, hidden_half:], 1)
    grad_got, hidden_other = lax.optimization_barrier((grad_got, hidden_other))

    token_part, rows, left = local_call(
        functools.partial(backward_kernel, blocks, capacity),
        [(unit_shape, BF16), (row_shape, BF16), ((rank, inner), F32)],
        scratch
        + [
            pltpu.VMEM((2, slots, inner), BF16),
            pltpu.VMEM((rank, width), F32),
            pltpu.VMEM((rank, hidden_half), F32),
            pltpu.VMEM((rank, inner), F32),
        ],
        grad_got, act, act_slope, hidden, q_full, error_left, weights,
        hbm=range(7), out_hbm=range(3), memory=58,
    )
    slot_grad = exchange(token_part)
    token_grad = dot(spread, slot_grad, NN).astype(BF16)
    token_grad = jnp.concatenate(jnp.split(token_grad, PIECES, axis=0), axis=1)

    rows_all = lax.all_gather(rows, "half", axis=0, tiled=True)
    hidden_mine = hidden[:, :hidden_half]
    hidden_all = jnp.concatenate(
        [
            jnp.where(half == 0, hidden_mine, hidden_other),
            jnp.where(half == 0, hidden_other, hidden_mine),
        ],
        axis=0,
    )

    left = pairs_sum(lax.all_gather(left, ("across", "core")))
    near, far, both = moved(left, 8), moved(left, 1), moved(left, 9)
    left = left + near
    away = far + both
    left = left + jnp.concatenate([away[:, hidden_half:], away[:, :hidden_half]], axis=1)
    core = lax.axis_index("core")
    span = width // lax.axis_size("core")
    basis, right, right_away = local_call(
        basis_kernel,
        [
            ((rank, hidden_half), F32),
            ((rank, span), F32),
            ((rank, span), F32),
        ],
        [
            pltpu.VMEM(row_shape, BF16),
            pltpu.VMEM((hidden_half, width), BF16),
            pltpu.SemaphoreType.DMA((2,)),
        ],
        core.reshape(1), left, hidden, rows, error, hbm=(3, 4), smem=(0,),
    )
    right = (right + lax.ppermute(right_away, "core", [(0, 1), (1, 0)])).astype(BF16)
    right = lax.all_gather(right, ("across", "core"))
    right = pairs_sum(right.reshape(-1, 2, rank, span).astype(F32))
    right = right.transpose(1, 0, 2).reshape(rank, width)
    near, far, both = moved(right, 8), moved(right, 1), moved(right, 9)
    merged = dot(hidden_all, rows_all, TN) + error.astype(F32)
    replicas = lax.axis_size("along") * lax.axis_size("across") * lax.axis_size("core")
    right, token_grad = lax.optimization_barrier((right + near, token_grad))
    right = (right + (far + both)) / replicas
    (new_error,) = local_call(
        error_kernel, [((hidden_half, width), BF16)], [], merged, basis, right
    )
    q_columns = jnp.where(half == 0, right[: rank // 2], right[rank // 2 :])
    replica = lax.axis_index("along") * lax.axis_size("across") + lax.axis_index("across")
    replica = replica * lax.axis_size("core") + core
    q_rows = width // replicas
    q_factor = lax.dynamic_slice_in_dim(q_columns, replica * q_rows, q_rows, 1).T
    return token_grad, basis.T, q_factor, new_error


def solution(mesh):
    replicas, places = mesh.shape["dp"], mesh.shape["expert"]
    split = Mesh(
        mesh.devices.reshape(2, replicas // 4, 2, places // 2, 2),
        ("along", "across", "core", "expert", "half"),
    )
    pair = ("expert", "half")
    rows = P(DP + pair, None)
    in_specs = (rows, rows, rows, rows, P(DP, pair), P(DP, pair), P(pair, DP), rows, P(None, pair))
    out_specs = (rows, P(pair, None), P(DP, pair), rows)
    return jax.shard_map(shards, mesh=split, in_specs=in_specs, out_specs=out_specs, check_vma=False)
```

```python
import functools

import jax
import jax.numpy as jnp
from jax import lax
from jax.experimental import pallas as pl
from jax.experimental.pallas import tpu as pltpu
from jax.sharding import Mesh
from jax.sharding import PartitionSpec as P

HIGHEST = lax.Precision.HIGHEST
BF16, F32 = jnp.bfloat16, jnp.float32
PIECES = 2
BLOCK = 4
BLOCKS = 3
NN = ((1,), (0,))
NT = ((1,), (1,))
TN = ((0,), (0,))
DP = ("along", "across", "core")
PLANE = ("along", "across", "half")


def dot(left, right, dims, precision=None):
    return lax.dot_general(
        left, right, (dims, ((), ())), precision=precision, preferred_element_type=F32
    )


def thirds(value):
    high = value.astype(BF16)
    rest = value - high.astype(F32)
    middle = rest.astype(BF16)
    low = (rest - middle.astype(F32)).astype(BF16)
    return jnp.concatenate([high, middle, low], axis=0)


def folded(value):
    rows = value.shape[0] // 3
    return value[:rows] + value[rows : 2 * rows] + value[2 * rows :]


def local_call(kernel, outs, scratch, *operands, hbm=(), out_hbm=(), memory=16, smem=()):
    def specs(count, there, scalars=()):
        spaces = [pltpu.HBM if i in there else pltpu.VMEM for i in range(count)]
        spaces = [pltpu.SMEM if i in scalars else space for i, space in enumerate(spaces)]
        return [pl.BlockSpec(memory_space=space) for space in spaces]

    return pl.pallas_call(
        kernel,
        out_shape=[jax.ShapeDtypeStruct(shape, dtype) for shape, dtype in outs],
        in_specs=specs(len(operands), hbm, smem),
        out_specs=specs(len(outs), out_hbm),
        scratch_shapes=scratch,
        compiler_params=pltpu.CompilerParams(vmem_limit_bytes=memory * 2**20),
    )(*operands)


def sides_of(array, width):
    return [array.at[:, pl.ds(side * width, width)] for side in range(2)]


def blocks_of(array, rows):
    return [array.at[pl.ds(i * rows, rows), :] for i in range(array.shape[0] // rows)]


def copies_of(sources, targets, sems, first):
    return [
        pltpu.make_async_copy(source, target, sems.at[first + i])
        for i, (source, target) in enumerate(zip(sources, targets))
    ]


def started(copies):
    for copy in copies:
        copy.start()


def finished(copies):
    for copy in copies:
        copy.wait()


def weight_copies(w_ref, proj_ref, down_ref, sems, half):
    proj, down = [], []
    for side in range(2):
        start = side * 3 * half
        proj.append(w_ref.at[:, pl.ds(start, 2 * half)])
        down.append(w_ref.at[:, pl.ds(start + 2 * half, half)])
    return (
        copies_of(proj, [proj_ref.at[side] for side in range(2)], sems, 0),
        copies_of(down, [down_ref.at[side] for side in range(2)], sems, 2),
    )


def reorder(count, capacity, dim):
    rows = lax.broadcasted_iota(jnp.int32, (count, count), dim)
    part = count // PIECES
    pieces = sum((rows >= part * j).astype(jnp.int32) for j in range(1, PIECES))
    inside = rows - part * pieces
    experts = sum(
        (inside >= capacity * i).astype(jnp.int32) for i in range(1, part // capacity)
    )
    place = inside - capacity * experts + capacity * pieces + PIECES * capacity * experts
    return (place == lax.broadcasted_iota(jnp.int32, (count, count), 1 - dim)).astype(BF16)


def to_rows(units_ref, rows_ref, arrivals, capacity):
    piece = units_ref.shape[1]
    count = units_ref.shape[0] // len(arrivals)
    part = count // PIECES
    order = reorder(count, capacity, 0)
    for i, copy in enumerate(arrivals):
        copy.wait()
        block = dot(order, units_ref[i * count : (i + 1) * count, :], NN).astype(BF16)
        for j in range(PIECES):
            rows_ref[i * part : (i + 1) * part, j * piece : (j + 1) * piece] = block[
                j * part : (j + 1) * part
            ]


def to_units(rows_ref, units_ref, departures, capacity):
    piece = units_ref.shape[1]
    count = units_ref.shape[0] // len(departures)
    part = count // PIECES
    order = reorder(count, capacity, 1)
    for i, copy in enumerate(departures):
        block = jnp.concatenate(
            [
                rows_ref[i * part : (i + 1) * part, j * piece : (j + 1) * piece]
                for j in range(PIECES)
            ],
            axis=0,
        )
        units_ref[i * count : (i + 1) * count, :] = dot(order, block, NN).astype(BF16)
        copy.start()


def forward_kernel(
    blocks, capacity, got_hbm, w_hbm, units_hbm, hidden_hbm, act_hbm, slope_hbm,
    proj_ref, down_ref, got_ref, rows_ref, outs_ref, units_ref, act_ref, slope_ref, hidden_ref, sems,
):
    half = hidden_ref.shape[1] // 2
    piece = got_ref.shape[1]
    count = got_ref.shape[0] // blocks
    arrivals = copies_of(blocks_of(got_hbm, count), blocks_of(got_ref, count), sems, 12)
    departures = copies_of(
        blocks_of(units_ref, count), blocks_of(units_hbm, count), sems, 12 + blocks
    )
    proj, down = weight_copies(w_hbm, proj_ref, down_ref, sems, half)
    kept = copies_of(sides_of(act_ref, half), sides_of(act_hbm, half), sems, 4)
    kept += copies_of(sides_of(slope_ref, half), sides_of(slope_hbm, half), sems, 6)
    kept += copies_of(sides_of(hidden_ref, half), sides_of(hidden_hbm, half), sems, 8)
    started(arrivals + proj + down)
    to_rows(got_ref, rows_ref, arrivals, capacity)
    rows = rows_ref[...]
    for side in range(2):
        proj[side].wait()
        pre = dot(rows, proj_ref[side], NN)
        pre_gate, pre_up = pre[:, :half], pre[:, half:]
        sig = jax.nn.sigmoid(pre_gate)
        act = pre_gate * sig
        columns = slice(side * half, (side + 1) * half)
        hidden_ref[:, columns] = (act * pre_up).astype(BF16)
        act_ref[:, columns] = act
        slope_ref[:, columns] = pre_up * sig * (1.0 + pre_gate * (1.0 - sig))
        started(kept[side::2])
    finished(down)
    for j in range(PIECES):
        cols = slice(j * piece, (j + 1) * piece)
        out = dot(hidden_ref[:, :half], down_ref[0, cols, :], NT)
        out = out + dot(hidden_ref[:, half:], down_ref[1, cols, :], NT)
        outs_ref[:, cols] = out.astype(BF16)
    to_units(outs_ref, units_ref, departures, capacity)
    finished(kept + departures)


def backward_kernel(
    blocks, capacity, got_hbm, act_hbm, slope_hbm, hidden_hbm, q_hbm, error_left_hbm, w_hbm,
    units_hbm, rows_hbm, left_hbm,
    proj_ref, down_ref, got_ref, rows_ref, outs_ref, units_ref, act_ref, slope_ref, hidden_ref, sems,
    grads_ref, q_ref, error_left_ref, left_ref,
):
    half = act_ref.shape[1] // 2
    piece = units_ref.shape[1]
    count = got_ref.shape[0] // blocks
    arrivals = copies_of(blocks_of(got_hbm, count), blocks_of(got_ref, count), sems, 12)
    departures = copies_of(
        blocks_of(units_ref, count), blocks_of(units_hbm, count), sems, 12 + blocks
    )
    proj, down = weight_copies(w_hbm, proj_ref, down_ref, sems, half)
    kept = copies_of(sides_of(act_hbm, half), sides_of(act_ref, half), sems, 4)
    kept += copies_of(sides_of(slope_hbm, half), sides_of(slope_ref, half), sems, 6)
    small = copies_of([q_hbm, hidden_hbm], [q_ref, hidden_ref], sems, 8)
    small += copies_of([error_left_hbm], [error_left_ref], sems, 10)
    out_rows = copies_of([rows_ref], [rows_hbm], sems, 12 + 2 * blocks)
    out_left = copies_of([left_ref], [left_hbm], sems, 11)
    started(arrivals + small + down + kept + proj)
    to_rows(got_ref, rows_ref, arrivals, capacity)
    started(out_rows)
    rows = rows_ref[...]
    finished(small)
    grad_q = folded(dot(thirds(q_ref[...]), rows, NT))
    left = folded(dot(thirds(grad_q), hidden_ref[...], NN))
    left_ref[:, :half] = left[:, :half] + error_left_ref[...]
    left_ref[:, half:] = left[:, half:]
    started(out_left)
    for side in range(2):
        columns = slice(side * half, (side + 1) * half)
        down[side].wait()
        hidden_grad = dot(rows, down_ref[side], NN)
        kept[side].wait()
        kept[2 + side].wait()
        grads_ref[side, :, :half] = (hidden_grad * slope_ref[:, columns]).astype(BF16)
        grads_ref[side, :, half:] = (hidden_grad * act_ref[:, columns]).astype(BF16)
    finished(proj)
    for j in range(PIECES):
        cols = slice(j * piece, (j + 1) * piece)
        out = dot(grads_ref[0], proj_ref[0, cols, :], NT)
        out = out + dot(grads_ref[1], proj_ref[1, cols, :], NT)
        outs_ref[:, cols] = out.astype(BF16)
    to_units(outs_ref, units_ref, departures, capacity)
    finished(departures + out_rows + out_left)


def basis_kernel(
    core_ref, left_ref, hidden_ref, rows_hbm, error_hbm, basis_ref, right_ref, away_ref,
    rows_ref, error_ref, sems,
):
    copies = copies_of([rows_hbm, error_hbm], [rows_ref, error_ref], sems, 0)
    started(copies)
    left = left_ref[...]
    rank = left.shape[0]
    half = left.shape[1] // 2
    gram = dot(left, left, NT, HIGHEST)
    row_ids = lax.broadcasted_iota(jnp.int32, (rank, rank), 0)
    inverse = jnp.where(
        row_ids == lax.broadcasted_iota(jnp.int32, (rank, rank), 1), 1.0, 0.0
    ).astype(F32)
    for k in range(rank):
        scale = 1.0 / jnp.sqrt(gram[k : k + 1, k : k + 1])
        gram_row = gram[k : k + 1, :] * scale
        inverse_row = inverse[k : k + 1, :] * scale
        below = jnp.where(row_ids > k, gram[:, k : k + 1] * scale, 0.0)
        gram = gram - below * gram_row
        inverse = jnp.where(row_ids == k, inverse_row, inverse - below * inverse_row)
    basis = dot(inverse, left, NN, HIGHEST)
    mine = basis[:, :half]
    basis_ref[...] = mine
    terms = thirds(mine)
    finished(copies)
    hidden_basis = folded(dot(thirds(basis), hidden_ref[...], NT))
    right = folded(dot(terms, error_ref[...], NN))
    right = right + folded(dot(thirds(hidden_basis), rows_ref[...], NN))
    span = right_ref.shape[1]
    first = core_ref[0] == 0
    right_ref[...] = jnp.where(first, right[:, :span], right[:, span:])
    away_ref[...] = jnp.where(first, right[:, span:], right[:, :span])


def error_kernel(
    replicas, place_ref, merged_ref, basis_ref, right_ref, near_ref, far_ref, both_ref, error_hbm,
    fresh_hbm, factor_ref, error_ref, total_ref, fresh_ref, sems,
):
    rank, width = right_ref.shape
    count = merged_ref.shape[0] // BLOCKS
    arrivals = copies_of(blocks_of(error_hbm, count), blocks_of(error_ref, count), sems, 0)
    results = copies_of(blocks_of(fresh_ref, count), blocks_of(fresh_hbm, count), sems, BLOCKS)
    started(arrivals)
    right, near, far, both = (
        ref[...].astype(F32) for ref in (right_ref, near_ref, far_ref, both_ref)
    )
    total = ((right + near) + (far + both)) / replicas
    total_ref[...] = total
    span = width // replicas
    start = pl.multiple_of(place_ref[1] * span, span)
    columns = total_ref[:, pl.ds(start, span)]
    factor_ref[...] = jnp.where(place_ref[0] == 0, columns[: rank // 2], columns[rank // 2 :])
    basis, right = thirds(basis_ref[...]), thirds(total)
    high, middle = right[:rank], right[rank : 2 * rank]
    left = jnp.concatenate([basis[:rank], basis[:rank], basis[rank : 2 * rank]], axis=0)
    terms = jnp.concatenate([high, middle, high], axis=0)
    for i in range(BLOCKS):
        part = slice(i * count, (i + 1) * count)
        approx = dot(left[:, part], terms, TN)
        arrivals[i].wait()
        merged = merged_ref[part, :] + error_ref[part, :].astype(F32)
        fresh_ref[part, :] = (merged - approx).astype(BF16)
        results[i].start()
    finished(results)


def moved(value, mask):
    count = lax.axis_size("along") * lax.axis_size("across") * lax.axis_size("half")
    return lax.ppermute(value, PLANE, [(source, source ^ mask) for source in range(count)])


def pairs_sum(values):
    while values.shape[0] > 1:
        half = values.shape[0] // 2
        values = values[:half] + values[half:]
    return values[0]


def shards(tokens, target, routes, gates, w_gate, w_up, w_down, error, q_start):
    experts = lax.axis_size("expert")
    half = lax.axis_index("half")
    tok, width = tokens.shape
    top = routes.shape[1]
    hidden_half = w_gate.shape[1]
    inner = 2 * hidden_half
    capacity = max(2, min(tok, 2 * (5 * tok * top // (8 * experts))))
    piece = width // PIECES
    unit = PIECES * capacity
    slots = experts * capacity
    rank = 2 * q_start.shape[1]

    own = jnp.concatenate([w_gate, w_up, w_down.T], axis=1)
    packed = jnp.concatenate([own, moved(own, 1)], axis=1)

    expert_ids = jnp.arange(experts, dtype=jnp.int32)
    hits = (routes[:, :, None] == expert_ids).astype(jnp.int32)
    per_token = jnp.sum(hits, axis=1)
    earlier = jnp.cumsum(per_token, axis=0) - per_token
    position = jnp.sum(hits * earlier[:, None, :], axis=2)
    base = (routes * unit + position).T
    lanes = jnp.arange(experts * unit, dtype=jnp.int32)
    places = jnp.arange(PIECES, dtype=jnp.int32)[:, None, None] * capacity + base
    select = (places[..., None] == lanes).astype(BF16)
    spread = jnp.sum(select, axis=1).reshape(PIECES * tok, experts * unit)
    select = select.reshape(PIECES * top * tok, experts * unit)

    def pieces_of(rows):
        return jnp.concatenate(jnp.split(rows, PIECES, axis=-1), axis=0)

    def exchange(rows):
        sent = rows.reshape(experts, unit, piece)
        back = lax.all_to_all(sent, "expert", split_axis=0, concat_axis=0, tiled=True)
        return back.reshape(experts * unit, piece)

    send = dot(spread, pieces_of(tokens), TN).astype(BF16)
    packed, send = lax.optimization_barrier((packed, send))
    weights = lax.all_gather(packed, DP, axis=0, tiled=True)
    inbox = exchange(send)

    q_mine = q_start.T
    q_other = moved(q_mine, 1)
    q_full = jnp.concatenate(
        [jnp.where(half == 0, q_mine, q_other), jnp.where(half == 0, q_other, q_mine)], axis=0
    )
    error_left = dot(q_full, error.astype(F32), NT, HIGHEST)
    inbox, q_full, error_left = lax.optimization_barrier((inbox, q_full, error_left))

    unit_shape, row_shape = (experts * unit, piece), (slots, width)
    blocks = experts // min(BLOCK, experts)
    scratch = [
        pltpu.VMEM((2, width, inner), BF16),
        pltpu.VMEM((2, width, hidden_half), BF16),
        pltpu.VMEM(unit_shape, BF16),
        pltpu.VMEM(row_shape, BF16),
        pltpu.VMEM(row_shape, BF16),
        pltpu.VMEM(unit_shape, BF16),
        pltpu.VMEM((slots, inner), F32),
        pltpu.VMEM((slots, inner), F32),
        pltpu.VMEM((slots, inner), BF16),
        pltpu.SemaphoreType.DMA((13 + 2 * blocks,)),
    ]
    returned, hidden, act, act_slope = local_call(
        functools.partial(forward_kernel, blocks, capacity),
        [(unit_shape, BF16), ((slots, inner), BF16), ((slots, inner), F32), ((slots, inner), F32)],
        scratch,
        inbox, weights, hbm=(0, 1), out_hbm=(0, 1, 2, 3), memory=54,
    )
    returned = exchange(returned)
    picked = dot(select, returned, NN).reshape(PIECES, top, tok, piece)
    gate = gates.T[None, :, :, None]
    layer_sum = jnp.sum(gate * picked, axis=1)
    slope = layer_sum - pieces_of(target).reshape(PIECES, tok, piece).astype(F32)
    out_grad = (gate * slope[:, None]).astype(BF16).reshape(PIECES * top * tok, piece)
    grad_got = exchange(dot(select, out_grad, TN).astype(BF16))
    hidden_other = moved(hidden[:, hidden_half:], 1)
    hidden_mine = hidden[:, :hidden_half]
    hidden_all = jnp.concatenate(
        [
            jnp.where(half == 0, hidden_mine, hidden_other),
            jnp.where(half == 0, hidden_other, hidden_mine),
        ],
        axis=0,
    )
    grad_got, hidden_all = lax.optimization_barrier((grad_got, hidden_all))

    token_part, rows, left = local_call(
        functools.partial(backward_kernel, blocks, capacity),
        [(unit_shape, BF16), (row_shape, BF16), ((rank, inner), F32)],
        scratch
        + [
            pltpu.VMEM((2, slots, inner), BF16),
            pltpu.VMEM((rank, width), F32),
            pltpu.VMEM((rank, hidden_half), F32),
            pltpu.VMEM((rank, inner), F32),
        ],
        grad_got, act, act_slope, hidden, q_full, error_left, weights,
        hbm=range(7), out_hbm=range(3), memory=52,
    )
    slot_grad = exchange(token_part)
    token_grad = dot(spread, slot_grad, NN).astype(BF16)
    token_grad = jnp.concatenate(jnp.split(token_grad, PIECES, axis=0), axis=1)

    rows_all = lax.all_gather(rows, "half", axis=0, tiled=True)

    near, far, both = moved(left, 8), moved(left, 1), moved(left, 9)
    away = far + both
    left = (left + near) + jnp.concatenate([away[:, hidden_half:], away[:, :hidden_half]], axis=1)
    left = pairs_sum(lax.all_gather(left, ("across", "core")))
    core = lax.axis_index("core")
    span = width // lax.axis_size("core")
    basis, right, right_away = local_call(
        basis_kernel,
        [
            ((rank, hidden_half), F32),
            ((rank, span), F32),
            ((rank, span), F32),
        ],
        [
            pltpu.VMEM(row_shape, BF16),
            pltpu.VMEM((hidden_half, width), BF16),
            pltpu.SemaphoreType.DMA((2,)),
        ],
        core.reshape(1), left, hidden, rows, error, hbm=(3, 4), smem=(0,),
    )
    right = (right + lax.ppermute(right_away, "core", [(0, 1), (1, 0)])).astype(BF16)
    right = lax.all_gather(right, ("across", "core"))
    right = right.reshape(-1, 2, rank, span).astype(F32).sum(axis=0)
    right = jnp.concatenate([right[0], right[1]], axis=1).astype(BF16)
    near, far, both = moved(right, 8), moved(right, 1), moved(right, 9)
    merged = dot(hidden_all, rows_all, TN)
    replicas = lax.axis_size("along") * lax.axis_size("across") * lax.axis_size("core")
    near, token_grad = lax.optimization_barrier((near, token_grad))
    replica = lax.axis_index("along") * lax.axis_size("across") + lax.axis_index("across")
    replica = replica * lax.axis_size("core") + core
    new_error, q_factor = local_call(
        functools.partial(error_kernel, replicas),
        [((hidden_half, width), BF16), ((rank // 2, width // replicas), F32)],
        [
            pltpu.VMEM((hidden_half, width), BF16),
            pltpu.VMEM((rank, width), F32),
            pltpu.VMEM((hidden_half, width), BF16),
            pltpu.SemaphoreType.DMA((2 * BLOCKS,)),
        ],
        jnp.stack([half, replica]), merged, basis, right, near, far, both, error,
        smem=(0,), hbm=(7,), out_hbm=(0,),
    )
    return token_grad, basis.T, q_factor.T, new_error


def solution(mesh):
    replicas, places = mesh.shape["dp"], mesh.shape["expert"]
    split = Mesh(
        mesh.devices.reshape(2, replicas // 4, 2, places // 2, 2),
        ("along", "across", "core", "expert", "half"),
    )
    pair = ("expert", "half")
    rows = P(DP + pair, None)
    in_specs = (rows, rows, rows, rows, P(DP, pair), P(DP, pair), P(pair, DP), rows, P(None, pair))
    out_specs = (rows, P(pair, None), P(DP, pair), rows)
    return jax.shard_map(shards, mesh=split, in_specs=in_specs, out_specs=out_specs, check_vma=False)
```

```python
import functools

import jax
import jax.numpy as jnp
from jax import lax
from jax.experimental import pallas as pl
from jax.experimental.pallas import tpu as pltpu
from jax.sharding import Mesh
from jax.sharding import PartitionSpec as P

HIGHEST = lax.Precision.HIGHEST
BF16, F32 = jnp.bfloat16, jnp.float32
PIECES = 2
BLOCK = 4
BLOCKS = 3
NN = ((1,), (0,))
NT = ((1,), (1,))
TN = ((0,), (0,))
DP = ("along", "across", "core")
PLANE = ("along", "across", "half")


def dot(left, right, dims, precision=None):
    return lax.dot_general(
        left, right, (dims, ((), ())), precision=precision, preferred_element_type=F32
    )


def thirds(value):
    high = value.astype(BF16)
    rest = value - high.astype(F32)
    middle = rest.astype(BF16)
    low = (rest - middle.astype(F32)).astype(BF16)
    return jnp.concatenate([high, middle, low], axis=0)


def folded(value):
    rows = value.shape[0] // 3
    return value[:rows] + value[rows : 2 * rows] + value[2 * rows :]


def local_call(kernel, outs, scratch, *operands, hbm=(), out_hbm=(), memory=16, smem=()):
    def specs(count, there, scalars=()):
        spaces = [pltpu.HBM if i in there else pltpu.VMEM for i in range(count)]
        spaces = [pltpu.SMEM if i in scalars else space for i, space in enumerate(spaces)]
        return [pl.BlockSpec(memory_space=space) for space in spaces]

    return pl.pallas_call(
        kernel,
        out_shape=[jax.ShapeDtypeStruct(shape, dtype) for shape, dtype in outs],
        in_specs=specs(len(operands), hbm, smem),
        out_specs=specs(len(outs), out_hbm),
        scratch_shapes=scratch,
        compiler_params=pltpu.CompilerParams(vmem_limit_bytes=memory * 2**20),
    )(*operands)


def sides_of(array, width):
    return [array.at[:, pl.ds(side * width, width)] for side in range(2)]


def blocks_of(array, rows):
    return [array.at[pl.ds(i * rows, rows), :] for i in range(array.shape[0] // rows)]


def copies_of(sources, targets, sems, first):
    return [
        pltpu.make_async_copy(source, target, sems.at[first + i])
        for i, (source, target) in enumerate(zip(sources, targets))
    ]


def started(copies):
    for copy in copies:
        copy.start()


def finished(copies):
    for copy in copies:
        copy.wait()


def weight_copies(w_ref, proj_ref, down_ref, sems, half):
    proj, down = [], []
    for side in range(2):
        start = side * 3 * half
        proj.append(w_ref.at[:, pl.ds(start, 2 * half)])
        down.append(w_ref.at[:, pl.ds(start + 2 * half, half)])
    return (
        copies_of(proj, [proj_ref.at[side] for side in range(2)], sems, 0),
        copies_of(down, [down_ref.at[side] for side in range(2)], sems, 2),
    )


def reorder(count, capacity, dim):
    rows = lax.broadcasted_iota(jnp.int32, (count, count), dim)
    part = count // PIECES
    pieces = sum((rows >= part * j).astype(jnp.int32) for j in range(1, PIECES))
    inside = rows - part * pieces
    experts = sum(
        (inside >= capacity * i).astype(jnp.int32) for i in range(1, part // capacity)
    )
    place = inside - capacity * experts + capacity * pieces + PIECES * capacity * experts
    return (place == lax.broadcasted_iota(jnp.int32, (count, count), 1 - dim)).astype(BF16)


def to_rows(units_ref, rows_ref, arrivals, capacity):
    piece = units_ref.shape[1]
    count = units_ref.shape[0] // len(arrivals)
    part = count // PIECES
    order = reorder(count, capacity, 0)
    for i, copy in enumerate(arrivals):
        copy.wait()
        block = dot(order, units_ref[i * count : (i + 1) * count, :], NN).astype(BF16)
        for j in range(PIECES):
            rows_ref[i * part : (i + 1) * part, j * piece : (j + 1) * piece] = block[
                j * part : (j + 1) * part
            ]


def to_units(rows_ref, units_ref, departures, capacity):
    piece = units_ref.shape[1]
    count = units_ref.shape[0] // len(departures)
    part = count // PIECES
    order = reorder(count, capacity, 1)
    for i, copy in enumerate(departures):
        block = jnp.concatenate(
            [
                rows_ref[i * part : (i + 1) * part, j * piece : (j + 1) * piece]
                for j in range(PIECES)
            ],
            axis=0,
        )
        units_ref[i * count : (i + 1) * count, :] = dot(order, block, NN).astype(BF16)
        copy.start()


def forward_kernel(
    blocks, capacity, got_hbm, w_hbm, units_hbm, hidden_hbm, act_hbm, slope_hbm,
    proj_ref, down_ref, got_ref, rows_ref, outs_ref, units_ref, act_ref, slope_ref, hidden_ref, sems,
):
    half = hidden_ref.shape[1] // 2
    piece = got_ref.shape[1]
    count = got_ref.shape[0] // blocks
    arrivals = copies_of(blocks_of(got_hbm, count), blocks_of(got_ref, count), sems, 12)
    departures = copies_of(
        blocks_of(units_ref, count), blocks_of(units_hbm, count), sems, 12 + blocks
    )
    proj, down = weight_copies(w_hbm, proj_ref, down_ref, sems, half)
    kept = copies_of(sides_of(act_ref, half), sides_of(act_hbm, half), sems, 4)
    kept += copies_of(sides_of(slope_ref, half), sides_of(slope_hbm, half), sems, 6)
    kept += copies_of(sides_of(hidden_ref, half), sides_of(hidden_hbm, half), sems, 8)
    started(arrivals + proj + down)
    to_rows(got_ref, rows_ref, arrivals, capacity)
    rows = rows_ref[...]
    for side in range(2):
        proj[side].wait()
        pre = dot(rows, proj_ref[side], NN)
        pre_gate, pre_up = pre[:, :half], pre[:, half:]
        sig = jax.nn.sigmoid(pre_gate)
        act = pre_gate * sig
        columns = slice(side * half, (side + 1) * half)
        hidden_ref[:, columns] = (act * pre_up).astype(BF16)
        act_ref[:, columns] = act
        slope_ref[:, columns] = pre_up * sig * (1.0 + pre_gate * (1.0 - sig))
        started(kept[side::2])
    finished(down)
    for j in range(PIECES):
        cols = slice(j * piece, (j + 1) * piece)
        out = dot(hidden_ref[:, :half], down_ref[0, cols, :], NT)
        out = out + dot(hidden_ref[:, half:], down_ref[1, cols, :], NT)
        outs_ref[:, cols] = out.astype(BF16)
    to_units(outs_ref, units_ref, departures, capacity)
    finished(kept + departures)


def backward_kernel(
    blocks, capacity, got_hbm, act_hbm, slope_hbm, hidden_hbm, q_hbm, error_left_hbm, w_hbm,
    units_hbm, rows_hbm, left_hbm,
    proj_ref, down_ref, got_ref, rows_ref, outs_ref, units_ref, act_ref, slope_ref, hidden_ref, sems,
    grads_ref, q_ref, error_left_ref, left_ref,
):
    half = act_ref.shape[1] // 2
    piece = units_ref.shape[1]
    count = got_ref.shape[0] // blocks
    arrivals = copies_of(blocks_of(got_hbm, count), blocks_of(got_ref, count), sems, 12)
    departures = copies_of(
        blocks_of(units_ref, count), blocks_of(units_hbm, count), sems, 12 + blocks
    )
    proj, down = weight_copies(w_hbm, proj_ref, down_ref, sems, half)
    kept = copies_of(sides_of(act_hbm, half), sides_of(act_ref, half), sems, 4)
    kept += copies_of(sides_of(slope_hbm, half), sides_of(slope_ref, half), sems, 6)
    small = copies_of([q_hbm, hidden_hbm], [q_ref, hidden_ref], sems, 8)
    small += copies_of([error_left_hbm], [error_left_ref], sems, 10)
    out_rows = copies_of([rows_ref], [rows_hbm], sems, 12 + 2 * blocks)
    out_left = copies_of([left_ref], [left_hbm], sems, 11)
    started(arrivals + small + down + kept + proj)
    to_rows(got_ref, rows_ref, arrivals, capacity)
    started(out_rows)
    rows = rows_ref[...]
    finished(small)
    grad_q = folded(dot(thirds(q_ref[...]), rows, NT))
    left = folded(dot(thirds(grad_q), hidden_ref[...], NN))
    left_ref[:, :half] = left[:, :half] + error_left_ref[...]
    left_ref[:, half:] = left[:, half:]
    started(out_left)
    for side in range(2):
        columns = slice(side * half, (side + 1) * half)
        down[side].wait()
        hidden_grad = dot(rows, down_ref[side], NN)
        kept[side].wait()
        kept[2 + side].wait()
        grads_ref[side, :, :half] = (hidden_grad * slope_ref[:, columns]).astype(BF16)
        grads_ref[side, :, half:] = (hidden_grad * act_ref[:, columns]).astype(BF16)
    finished(proj)
    for j in range(PIECES):
        cols = slice(j * piece, (j + 1) * piece)
        out = dot(grads_ref[0], proj_ref[0, cols, :], NT)
        out = out + dot(grads_ref[1], proj_ref[1, cols, :], NT)
        outs_ref[:, cols] = out.astype(BF16)
    to_units(outs_ref, units_ref, departures, capacity)
    finished(departures + out_rows + out_left)


def basis_kernel(
    core_ref, left_ref, hidden_ref, rows_hbm, error_hbm, basis_ref, right_ref, away_ref,
    rows_ref, error_ref, sems,
):
    copies = copies_of([rows_hbm, error_hbm], [rows_ref, error_ref], sems, 0)
    started(copies)
    left = left_ref[...]
    rank = left.shape[0]
    half = left.shape[1] // 2
    gram = dot(left, left, NT, HIGHEST)
    row_ids = lax.broadcasted_iota(jnp.int32, (rank, 2 * rank), 0)
    column_ids = lax.broadcasted_iota(jnp.int32, (rank, 2 * rank), 1)
    identity = jnp.where(row_ids + rank == column_ids, 1.0, 0.0).astype(F32)
    work = jnp.concatenate([gram, identity[:, rank:]], axis=1)
    for k in range(rank - 1):
        below = work[:, k : k + 1] / work[k : k + 1, k : k + 1]
        work = work - jnp.where(row_ids > k, below * work[k : k + 1, :], 0.0)
    pivots = jnp.sum(jnp.where(row_ids == column_ids, work, 0.0), axis=1, keepdims=True)
    inverse = work[:, rank:] / jnp.sqrt(pivots)
    basis = dot(inverse, left, NN, HIGHEST)
    mine = basis[:, :half]
    basis_ref[...] = mine
    terms = thirds(mine)
    finished(copies)
    hidden_basis = folded(dot(thirds(basis), hidden_ref[...], NT))
    right = folded(dot(terms, error_ref[...], NN))
    right = right + folded(dot(thirds(hidden_basis), rows_ref[...], NN))
    span = right_ref.shape[1]
    first = core_ref[0] == 0
    right_ref[...] = jnp.where(first, right[:, :span], right[:, span:])
    away_ref[...] = jnp.where(first, right[:, span:], right[:, :span])


def error_kernel(
    replicas, place_ref, grad_ref, basis_ref, right_ref, near_ref, far_ref, both_ref, error_hbm,
    fresh_hbm, factor_ref, error_ref, total_ref, fresh_ref, sems,
):
    rank, width = right_ref.shape
    count = grad_ref.shape[0] // BLOCKS
    arrivals = copies_of(blocks_of(error_hbm, count), blocks_of(error_ref, count), sems, 0)
    results = copies_of(blocks_of(fresh_ref, count), blocks_of(fresh_hbm, count), sems, BLOCKS)
    started(arrivals)
    right, near, far, both = (
        ref[...].astype(F32) for ref in (right_ref, near_ref, far_ref, both_ref)
    )
    total = ((right + near) + (far + both)) / replicas
    total_ref[...] = total
    span = width // replicas
    start = pl.multiple_of(place_ref[1] * span, span)
    columns = total_ref[:, pl.ds(start, span)]
    factor_ref[...] = jnp.where(place_ref[0] == 0, columns[: rank // 2], columns[rank // 2 :])
    basis, right = thirds(basis_ref[...]), thirds(total)
    high, middle = right[:rank], right[rank : 2 * rank]
    left = jnp.concatenate([basis[:rank], basis[:rank], basis[rank : 2 * rank]], axis=0)
    terms = jnp.concatenate([high, middle, high], axis=0)
    for i in range(BLOCKS):
        part = slice(i * count, (i + 1) * count)
        approx = dot(left[:, part], terms, TN)
        arrivals[i].wait()
        merged = grad_ref[part, :].astype(F32) + error_ref[part, :].astype(F32)
        fresh_ref[part, :] = (merged - approx).astype(BF16)
        results[i].start()
    finished(results)


def moved(value, mask):
    count = lax.axis_size("along") * lax.axis_size("across") * lax.axis_size("half")
    return lax.ppermute(value, PLANE, [(source, source ^ mask) for source in range(count)])


def pairs_sum(values):
    while values.shape[0] > 1:
        half = values.shape[0] // 2
        values = values[:half] + values[half:]
    return values[0]


def shards(tokens, target, routes, gates, w_gate, w_up, w_down, error, q_start):
    experts = lax.axis_size("expert")
    half = lax.axis_index("half")
    tok, width = tokens.shape
    top = routes.shape[1]
    hidden_half = w_gate.shape[1]
    inner = 2 * hidden_half
    capacity = max(2, min(tok, 2 * (5 * tok * top // (8 * experts))))
    piece = width // PIECES
    unit = PIECES * capacity
    slots = experts * capacity
    rank = 2 * q_start.shape[1]

    own = jnp.concatenate([w_gate, w_up, w_down.T], axis=1)
    packed = jnp.concatenate([own, moved(own, 1)], axis=1)

    expert_ids = jnp.arange(experts, dtype=jnp.int32)
    hits = (routes[:, :, None] == expert_ids).astype(jnp.int32)
    per_token = jnp.sum(hits, axis=1)
    earlier = jnp.cumsum(per_token, axis=0) - per_token
    position = jnp.sum(hits * earlier[:, None, :], axis=2)
    base = (routes * unit + position).T
    lanes = jnp.arange(experts * unit, dtype=jnp.int32)
    places = jnp.arange(PIECES, dtype=jnp.int32)[:, None, None] * capacity + base
    select = (places[..., None] == lanes).astype(BF16)
    spread = jnp.sum(select, axis=1).reshape(PIECES * tok, experts * unit)
    select = select.reshape(PIECES * top * tok, experts * unit)

    def pieces_of(rows):
        return jnp.concatenate(jnp.split(rows, PIECES, axis=-1), axis=0)

    def exchange(rows):
        sent = rows.reshape(experts, unit, piece)
        back = lax.all_to_all(sent, "expert", split_axis=0, concat_axis=0, tiled=True)
        return back.reshape(experts * unit, piece)

    send = dot(spread, pieces_of(tokens), TN).astype(BF16)
    packed, send = lax.optimization_barrier((packed, send))
    weights = lax.all_gather(packed, DP, axis=0, tiled=True)
    inbox = exchange(send)

    q_mine = q_start.T
    q_other = moved(q_mine, 1)
    q_full = jnp.concatenate(
        [jnp.where(half == 0, q_mine, q_other), jnp.where(half == 0, q_other, q_mine)], axis=0
    )
    error_left = dot(q_full, error.astype(F32), NT, HIGHEST)
    inbox, q_full, error_left = lax.optimization_barrier((inbox, q_full, error_left))

    unit_shape, row_shape = (experts * unit, piece), (slots, width)
    blocks = experts // min(BLOCK, experts)
    scratch = [
        pltpu.VMEM((2, width, inner), BF16),
        pltpu.VMEM((2, width, hidden_half), BF16),
        pltpu.VMEM(unit_shape, BF16),
        pltpu.VMEM(row_shape, BF16),
        pltpu.VMEM(row_shape, BF16),
        pltpu.VMEM(unit_shape, BF16),
        pltpu.VMEM((slots, inner), F32),
        pltpu.VMEM((slots, inner), F32),
        pltpu.VMEM((slots, inner), BF16),
        pltpu.SemaphoreType.DMA((13 + 2 * blocks,)),
    ]
    returned, hidden, act, act_slope = local_call(
        functools.partial(forward_kernel, blocks, capacity),
        [(unit_shape, BF16), ((slots, inner), BF16), ((slots, inner), F32), ((slots, inner), F32)],
        scratch,
        inbox, weights, hbm=(0, 1), out_hbm=(0, 1, 2, 3), memory=54,
    )
    returned = exchange(returned)
    picked = dot(select, returned, NN).reshape(PIECES, top, tok, piece)
    gate = gates.T[None, :, :, None]
    layer_sum = jnp.sum(gate * picked, axis=1)
    slope = layer_sum - pieces_of(target).reshape(PIECES, tok, piece).astype(F32)
    out_grad = (gate * slope[:, None]).astype(BF16).reshape(PIECES * top * tok, piece)
    grad_got = exchange(dot(select, out_grad, TN).astype(BF16))
    hidden_other = moved(hidden[:, hidden_half:], 1)
    hidden_mine = hidden[:, :hidden_half]
    hidden_all = jnp.concatenate(
        [
            jnp.where(half == 0, hidden_mine, hidden_other),
            jnp.where(half == 0, hidden_other, hidden_mine),
        ],
        axis=0,
    )
    grad_got, hidden_all = lax.optimization_barrier((grad_got, hidden_all))

    token_part, rows, left = local_call(
        functools.partial(backward_kernel, blocks, capacity),
        [(unit_shape, BF16), (row_shape, BF16), ((rank, inner), F32)],
        scratch
        + [
            pltpu.VMEM((2, slots, inner), BF16),
            pltpu.VMEM((rank, width), F32),
            pltpu.VMEM((rank, hidden_half), F32),
            pltpu.VMEM((rank, inner), F32),
        ],
        grad_got, act, act_slope, hidden, q_full, error_left, weights,
        hbm=range(7), out_hbm=range(3), memory=52,
    )
    slot_grad = exchange(token_part)
    token_grad = dot(spread, slot_grad, NN).astype(BF16)
    token_grad = jnp.concatenate(jnp.split(token_grad, PIECES, axis=0), axis=1)

    rows_all = lax.all_gather(rows, "half", axis=0, tiled=True)

    near, far, both = moved(left, 8), moved(left, 1), moved(left, 9)
    away = far + both
    left = (left + near) + jnp.concatenate([away[:, hidden_half:], away[:, :hidden_half]], axis=1)
    left = pairs_sum(lax.all_gather(left, ("across", "core")))
    core = lax.axis_index("core")
    span = width // lax.axis_size("core")
    basis, right, right_away = local_call(
        basis_kernel,
        [
            ((rank, hidden_half), F32),
            ((rank, span), F32),
            ((rank, span), F32),
        ],
        [
            pltpu.VMEM(row_shape, BF16),
            pltpu.VMEM((hidden_half, width), BF16),
            pltpu.SemaphoreType.DMA((2,)),
        ],
        core.reshape(1), left, hidden, rows, error, hbm=(3, 4), smem=(0,),
    )
    right = (right + lax.ppermute(right_away, "core", [(0, 1), (1, 0)])).astype(BF16)
    right = lax.all_gather(right, ("across", "core"))
    right = right.reshape(-1, 2, rank, span).astype(F32).sum(axis=0)
    right = jnp.concatenate([right[0], right[1]], axis=1).astype(BF16)
    near, far, both = moved(right, 8), moved(right, 1), moved(right, 9)
    weight_grad = dot(hidden_all, rows_all, TN).astype(BF16)
    replicas = lax.axis_size("along") * lax.axis_size("across") * lax.axis_size("core")
    near, token_grad = lax.optimization_barrier((near, token_grad))
    replica = lax.axis_index("along") * lax.axis_size("across") + lax.axis_index("across")
    replica = replica * lax.axis_size("core") + core
    new_error, q_factor = local_call(
        functools.partial(error_kernel, replicas),
        [((hidden_half, width), BF16), ((rank // 2, width // replicas), F32)],
        [
            pltpu.VMEM((hidden_half, width), BF16),
            pltpu.VMEM((rank, width), F32),
            pltpu.VMEM((hidden_half, width), BF16),
            pltpu.SemaphoreType.DMA((2 * BLOCKS,)),
        ],
        jnp.stack([half, replica]), weight_grad, basis, right, near, far, both, error,
        smem=(0,), hbm=(7,), out_hbm=(0,),
    )
    return token_grad, basis.T, q_factor.T, new_error


def solution(mesh):
    replicas, places = mesh.shape["dp"], mesh.shape["expert"]
    split = Mesh(
        mesh.devices.reshape(2, replicas // 4, 2, places // 2, 2),
        ("along", "across", "core", "expert", "half"),
    )
    pair = ("expert", "half")
    rows = P(DP + pair, None)
    in_specs = (rows, rows, rows, rows, P(DP, pair), P(DP, pair), P(pair, DP), rows, P(None, pair))
    out_specs = (rows, P(pair, None), P(DP, pair), rows)
    return jax.shard_map(shards, mesh=split, in_specs=in_specs, out_specs=out_specs, check_vma=False)
```
